32 devices in a mesh: groups: 2 (over x), dom: 16 (over z, y, core).
Axes of the slice: x: 2, y: 2, z: 4, core: 2. Of those that a mesh axis runs over, the one named last changes fastest.
Arguments:
- displacement: float32 [3, 69632], P(None, ('groups', 'dom')), parts along dimension 1, may hold values from -6 to 6
- velocity: float32 [3, 69632], P(None, ('groups', 'dom')), parts along dimension 1, may hold values from -6 to 6
- node_mass: float32 [69632], P(('groups', 'dom')), parts along dimension 0, may hold values from 0.5 to 2
- connectivity: int32 [8, 65536], P(None, ('groups', 'dom')), parts along dimension 1, may hold values from 0 to 2175
- modulus: float32 [65536], P(('groups', 'dom')), parts along dimension 0, may hold values from 0.3 to 1.2
- elem_stiffness: float32 [24, 24], replicated, as said below
- slave_nodes: int32 [2048, 128], P(('groups', 'dom')), parts along dimension 0, may hold values from 0 to 2175
- slave_gap: float32 [2048, 128], P(('groups', 'dom')), parts along dimension 0, may hold values from -6 to 6
- master_nodes: int32 [1024, 128], P(('groups', 'dom')), parts along dimension 0, may hold values from 0 to 2175
- pair_slave: int32 [4096], P(('groups', 'dom')), parts along dimension 0, may hold values from 0 to 63
- pair_owner: int32 [4096, 1], P(('groups', 'dom')), parts along dimension 0, may hold values from 0 to 15; in each aligned block of 128 rows (0 to 127, 128 to 255, ...) at most 16 rows name the same one
- pair_master: int32 [4096], P(('groups', 'dom')), parts along dimension 0, may hold values from 0 to 31
- pair_normal: float32 [3, 4096], P(None, ('groups', 'dom')), parts along dimension 1, may hold values from -4 to 4
- lower_face: int32 [16384], P(('groups', 'dom')), parts along dimension 0, may hold values from 0 to 2175
- upper_face: int32 [16384], P(('groups', 'dom')), parts along dimension 0, may hold values from 0 to 2175
- mortar: float32 [128, 128], replicated, as said below
Outputs:
- new_displacement: float32 [3, 69632], P(None, ('groups', 'dom')), parts along dimension 1
- new_velocity: float32 [3, 69632], P(None, ('groups', 'dom')), parts along dimension 1
The draws below stay inside these ranges and needn't reach their ends.
There are 2 independent parts, one for each index of `groups`. The reference program is written for one: setup_inputs(seed, part) draws one part's arguments, and reference() takes and returns one part's arrays. A program takes and returns all parts, laid end to end along the dimension named above; an argument that names none is the same for every part. Nothing has to cross between parts.
Inputs may be any that keep to these rules, and one draw needn't show every extreme that they name: `pair_owner`: in the 128 pairs of one partition at most 16 name the same owner, a bound that some block reaches. `elem_stiffness`: symmetric with a dominant positive diagonal. `mortar`: full rank with a positive diagonal.
All inputs are finite; a program needn't handle non-finite values.
Results may differ from the reference program's by a relative error of at most 0.0001.
Values sent between devices are 32-bit elements; how exact they have to be, the bound alone decides.
No kernel may reach another device: no remote copies, remote signals or barrier semaphores. Data moves between devices by JAX's collectives and lax.ppermute only.
A program may use at most 128 MiB of HBM per device.

```python
import math
import jax
import jax.numpy as jnp
import numpy as np
from jax import lax

ELEM_DEV = 2048
NODES_DEV = 2176
PATCH = 128
SP_DEV = 64
MP_DEV = 32
PAIRS_DEV = 128
CAP = 16
FACE_DEV = 512
STEPS = 3
NODES = 34816
ELEMS = 32768
SP_TOTAL = 1024
MP_TOTAL = 512
PAIRS = 2048
FACES = 8192
N_DOM = 16


def draw_elem_stiffness(key, part):
    key = jax.random.fold_in(key, 11)
    key_off, key_diag = jax.random.split(key)
    off = jax.random.normal(key_off, (24, 24), jnp.float32) * 0.3
    off = (off + off.T) * 0.5 * 0.25
    diagonal = jax.random.uniform(key_diag, (24,), jnp.float32, 1.0, 2.0)
    eye = jnp.eye(24, dtype=jnp.float32)
    return off * (1.0 - eye) + eye * diagonal[None, :]


def draw_mortar(key, part):
    key = jax.random.fold_in(key, 23)
    key_off, key_diag = jax.random.split(key)
    off = jax.random.normal(key_off, (PATCH, PATCH), jnp.float32) * 0.03
    diagonal = jax.random.uniform(key_diag, (PATCH,), jnp.float32, 0.6, 1.0)
    eye = jnp.eye(PATCH, dtype=jnp.float32)
    return off * (1.0 - eye) + eye * diagonal[None, :]


def set_ends(entries, rng, low, high):
    dims = entries.shape
    index_at = [jax.random.randint(jax.random.fold_in(rng, axis), (), 0, dims[axis]) for axis in range(len(dims))]
    entries = entries.at[tuple(index_at)].set(low)
    longest = dims.index(max(dims))
    index_at[longest] = (index_at[longest] + 1) % dims[longest]
    return entries.at[tuple(index_at)].set(high)


def steps_of(key, shape, shards, low, high):
    factor_of = 1.0
    for dim, parts in shards:
        steps = jax.random.uniform(jax.random.fold_in(jax.random.fold_in(key, 6), dim), (parts,), jnp.float32, low / len(shards), high / len(shards))
        factor_of = factor_of * jnp.repeat(jnp.exp(steps), shape[dim] // parts).reshape((-1,) + (1,) * (len(shape) - 1 - dim))
    return factor_of


def routed_block(rng, own, number, rows, amount, top, limit, skew):
    order = jax.random.permutation(rng, amount)
    crowded, common = shares(amount, rows * top, limit, skew, True), shares(amount, rows * top, limit, skew, False)
    places = jnp.arange(amount)

    def named(tallies, offset_by):
        used = int((tallies > 0).sum())
        fixed = max(1, used // 4)
        moved = fixed + (places - fixed + offset_by * (used - fixed)) % max(1, amount - fixed)
        return jnp.zeros((amount,), jnp.int32).at[order[jnp.where(places < fixed, places, moved)]].set(jnp.asarray(tallies, jnp.int32))

    tallies = jnp.where(number % 4 == 0, named(crowded, number // 4), named(common, number - number // 4 - 1))
    mixed = jax.random.permutation(jax.random.fold_in(own, 3), amount)
    giver, taker = mixed[0:amount // 2 * 2:2], mixed[1:amount // 2 * 2:2]
    margin = jnp.minimum(tallies[giver] - 1, limit - tallies[taker]) // 2
    margin = jnp.where((giver == order[0]) | (taker == order[0]) | (tallies[taker] == 0), 0, jnp.maximum(margin, 0))
    moved = jax.random.randint(jax.random.fold_in(own, 4), (amount // 2,), 0, 1 << 20) % (margin + 1)
    tallies = tallies.at[giver].add(-moved).at[taker].add(moved)
    members = jnp.searchsorted(jnp.cumsum(tallies), jnp.arange(rows * top), side="right").astype(jnp.int32)
    table = members.reshape(top, rows).T
    table = table[jax.random.permutation(jax.random.fold_in(own, 1), rows)]
    offset_by = jax.random.randint(jax.random.fold_in(own, 2), (rows, 1), 0, top)
    return jnp.take_along_axis(table, (jnp.arange(top)[None, :] + offset_by) % top, axis=1)


def shares(amount, total, reach, slope, full):
    weights = [(1 << 20) // math.isqrt(rank ** slope) + 1 for rank in range(1, amount + 1)]
    largest = reach if full else min(reach, max(-(-total // amount), total * weights[0] // sum(weights)))
    least = 1 if total - largest >= amount - 1 else 0
    holding, rest = [largest] + [least] * (amount - 1), total - largest - least * (amount - 1)
    while rest > 0:
        movable = [i for i in range(1, amount) if holding[i] < largest] or [i for i in range(1, amount) if holding[i] < reach]
        mass, remaining = sum([weights[i] for i in movable]), rest
        for i in movable:
            more = min(reach - holding[i], max(1, remaining * weights[i] // mass), rest)
            holding[i] = holding[i] + more
            rest = rest - more
    return np.array(holding)


def centred(stream_key, dims, deviation, reach, shards=(), held_as=jnp.bfloat16):
    loudness = steps_of(stream_key, dims, shards, -0.22, 0.18) if shards else 1.0
    entries = jax.random.normal(stream_key, dims, jnp.float32) * deviation * loudness
    return jnp.minimum(jnp.maximum(entries, -reach), reach).astype(held_as)


def setup_inputs(seed: int = 0, part: int = 0) -> dict:
    arg_keys = jax.random.split(jax.random.key(seed), 17)
    part_keys = jax.random.split(jax.random.fold_in(arg_keys[16], part), 17)
    displacement = centred(part_keys[0], (3, NODES), 1.0, 6.0, ((1, 16),), jnp.float32)
    velocity = centred(part_keys[1], (3, NODES), 1.0, 6.0, ((1, 16),), jnp.float32)
    node_mass = jnp.clip(jnp.exp(math.log(2.0) - 1.3862944 * jax.random.uniform(part_keys[2], (NODES,), jnp.float32) ** steps_of(part_keys[2], (NODES,), ((0, 16),), -0.2, 0.2)), 0.5, 2.0)
    connectivity = set_ends(jax.random.randint(part_keys[3], (8, ELEMS), 0, NODES_DEV), jax.random.fold_in(part_keys[3], 1), 0, NODES_DEV - 1).astype(jnp.int32)
    modulus = jnp.clip(jnp.exp(math.log(1.2) - 1.3862944 * jax.random.uniform(part_keys[4], (ELEMS,), jnp.float32) ** steps_of(part_keys[4], (ELEMS,), ((0, 16),), -0.2, 0.2)), 0.3, 1.2)
    elem_stiffness = draw_elem_stiffness(jax.random.fold_in(arg_keys[16], 71), part)
    slave_nodes = set_ends(jax.random.randint(part_keys[6], (SP_TOTAL, PATCH), 0, NODES_DEV), jax.random.fold_in(part_keys[6], 1), 0, NODES_DEV - 1).astype(jnp.int32)
    slave_gap = centred(part_keys[7], (SP_TOTAL, PATCH), 1.0, 6.0, ((0, 16),), jnp.float32)
    master_nodes = set_ends(jax.random.randint(part_keys[8], (MP_TOTAL, PATCH), 0, NODES_DEV), jax.random.fold_in(part_keys[8], 1), 0, NODES_DEV - 1).astype(jnp.int32)
    pair_slave = set_ends(jax.random.randint(part_keys[9], (PAIRS,), 0, SP_DEV), jax.random.fold_in(part_keys[9], 1), 0, SP_DEV - 1).astype(jnp.int32)
    pair_owner_keys = jax.random.split(jax.random.fold_in(part_keys[10], 1), PAIRS // PAIRS_DEV)
    pair_owner_turns = jax.random.permutation(jax.random.fold_in(part_keys[10], 3), PAIRS // PAIRS_DEV)
    pair_owner = jax.vmap(lambda own, number: routed_block(jax.random.fold_in(part_keys[10], 2), own, number, PAIRS_DEV, N_DOM, 1, CAP, 2))(pair_owner_keys, pair_owner_turns).reshape((PAIRS, 1))
    pair_master = set_ends(jax.random.randint(part_keys[11], (PAIRS,), 0, MP_DEV), jax.random.fold_in(part_keys[11], 1), 0, MP_DEV - 1).astype(jnp.int32)
    pair_normal = centred(part_keys[12], (3, PAIRS), 1.0, 4.0, ((1, 16),), jnp.float32)
    lower_face = set_ends(jax.random.randint(part_keys[13], (FACES,), 0, NODES_DEV), jax.random.fold_in(part_keys[13], 1), 0, NODES_DEV - 1).astype(jnp.int32)
    upper_face = set_ends(jax.random.randint(part_keys[14], (FACES,), 0, NODES_DEV), jax.random.fold_in(part_keys[14], 1), 0, NODES_DEV - 1).astype(jnp.int32)
    mortar = draw_mortar(jax.random.fold_in(arg_keys[16], 71), part)
    return dict(displacement=displacement, velocity=velocity, node_mass=node_mass, connectivity=connectivity, modulus=modulus, elem_stiffness=elem_stiffness, slave_nodes=slave_nodes, slave_gap=slave_gap, master_nodes=master_nodes, pair_slave=pair_slave, pair_owner=pair_owner, pair_master=pair_master, pair_normal=pair_normal, lower_face=lower_face, upper_face=upper_face, mortar=mortar)


time_step = 0.1


def reference(displacement, velocity, node_mass, connectivity, modulus, elem_stiffness, slave_nodes, slave_gap, master_nodes, pair_slave, pair_owner, pair_master, pair_normal, lower_face, upper_face, mortar):
    n_dom = N_DOM
    elem_dev = (jnp.arange(ELEMS, dtype=jnp.int32) // ELEM_DEV).astype(jnp.int32)
    conn_glob = connectivity + elem_dev[None, :] * NODES_DEV
    sp_dev = (jnp.arange(SP_TOTAL, dtype=jnp.int32) // SP_DEV).astype(jnp.int32)
    slave_glob = slave_nodes + sp_dev[:, None] * NODES_DEV
    mp_dev = (jnp.arange(MP_TOTAL, dtype=jnp.int32) // MP_DEV).astype(jnp.int32)
    master_glob = master_nodes + mp_dev[:, None] * NODES_DEV
    pair_dev = (jnp.arange(PAIRS, dtype=jnp.int32) // PAIRS_DEV).astype(jnp.int32)
    s_idx = pair_slave + pair_dev * SP_DEV
    m_idx = pair_master + pair_owner[:, 0] * MP_DEV
    face_dev = (jnp.arange(FACES, dtype=jnp.int32) // FACE_DEV).astype(jnp.int32)
    low_g = (lower_face + face_dev * NODES_DEV).reshape(n_dom, FACE_DEV)
    up_g = (upper_face + face_dev * NODES_DEV).reshape(n_dom, FACE_DEV)
    s_nodes = slave_glob[s_idx]
    m_nodes = master_glob[m_idx]
    gap0 = slave_gap[s_idx]
    normal = pair_normal.T
    u = displacement
    v = velocity
    for step in range(STEPS):
        ue = u[:, conn_glob].reshape(24, ELEMS)
        fe = jnp.dot(elem_stiffness, ue, precision=lax.Precision.HIGHEST) * modulus[None, :]
        elastic = jnp.zeros_like(u).at[:, conn_glob.reshape(-1)].add(fe.reshape(3, -1))
        us = jnp.moveaxis(u[:, s_nodes], 0, 1)
        um = jnp.moveaxis(u[:, m_nodes], 0, 1)
        mapped = jnp.einsum('ij,pcj->pci', mortar, um, precision=lax.Precision.HIGHEST)
        gap = gap0 + jnp.sum(normal[:, :, None] * (us - mapped), axis=1)
        press = jnp.maximum(-gap, 0.0)
        slave_force = press[:, None, :] * normal[:, :, None]
        master_force = -jnp.einsum('ij,pci->pcj', mortar, slave_force, precision=lax.Precision.HIGHEST)
        local = -elastic
        local = local.at[:, s_nodes.reshape(-1)].add(jnp.moveaxis(slave_force, 1, 0).reshape(3, -1))
        f_low = local[:, low_g]
        f_up = local[:, up_g]
        shared = local.at[:, low_g[1:].reshape(-1)].add(f_up[:, :-1].reshape(3, -1))
        shared = shared.at[:, up_g[:-1].reshape(-1)].add(f_low[:, 1:].reshape(3, -1))
        force = shared.at[:, m_nodes.reshape(-1)].add(jnp.moveaxis(master_force, 1, 0).reshape(3, -1))
        v = v + time_step * force / node_mass[None, :]
        u = u + time_step * v
    return u, v
```

```python
import functools

import jax
import jax.numpy as jnp
from jax import lax
from jax.experimental import pallas as pl
from jax.experimental.pallas import tpu as pltpu
from jax.sharding import PartitionSpec as P

LANES = 128
STEPS = 3
TIME_STEP = 0.1
SLOTS = 256
CHUNK = 16

F32 = jnp.float32
BF16 = jnp.bfloat16
HIGH = lax.Precision.HIGHEST
NN = (((1,), (0,)), ((), ()))
NT = (((1,), (1,)), ((), ()))
TN = (((0,), (0,)), ((), ()))

MAIN = 16
ROWS = 56
FACTOR_ROWS = 112


def dot_exact(a, b, dims):
    return lax.dot_general(a, b, dims, precision=HIGH, preferred_element_type=F32)


def iota(shape, dim):
    return lax.broadcasted_iota(jnp.int32, shape, dim)


def field_row(c, h):
    return c * MAIN + h if h < MAIN else 3 * MAIN + c


def to_field(flat_ref, field_ref):
    field_ref[...] = jnp.zeros_like(field_ref)
    for c in range(3):
        for h in range(MAIN + 1):
            r = field_row(c, h)
            field_ref[r : r + 1, :] = flat_ref[c : c + 1, h * LANES : (h + 1) * LANES]


def from_field(field, flat_ref):
    for c in range(3):
        for h in range(MAIN + 1):
            r = field_row(c, h)
            flat_ref[c : c + 1, h * LANES : (h + 1) * LANES] = field[r : r + 1, :]


def gather8(field_ref, index):
    lane = index & (LANES - 1)
    row = index >> 7
    found = [jnp.zeros((8, LANES), F32) for _ in range(3)]
    for h in range(MAIN + 1):
        here = row == h
        for c in range(3):
            r = field_row(c, h)
            table = jnp.broadcast_to(field_ref[r : r + 1, :], (8, LANES))
            value = jnp.take_along_axis(table, lane, axis=1, mode="promise_in_bounds")
            found[c] = jnp.where(here, value, found[c])
    return found


def scatter_factors(index, values, a_ref, b_ref, k):
    columns = slice(k * LANES, (k + 1) * LANES)
    i128 = iota((LANES, LANES), 0).astype(F32).astype(BF16)
    i16 = iota((16, LANES), 0).astype(F32).astype(BF16)
    lane = jnp.broadcast_to((index & (LANES - 1)).astype(F32), (LANES, LANES)).astype(BF16)
    row = jnp.broadcast_to((index >> 7).astype(F32), (16, LANES)).astype(BF16)
    one, zero = jnp.ones((LANES, LANES), BF16), jnp.zeros((LANES, LANES), BF16)
    b_ref[:, columns] = jnp.where(i128 == lane, one, zero)
    here = i16 == row
    zero16 = jnp.zeros((16, LANES), BF16)
    tail = zero16
    for c in range(3):
        high = values[c].astype(BF16).astype(F32)
        for s, part in enumerate((high, values[c] - high)):
            wide = jnp.broadcast_to(part, (16, LANES)).astype(BF16)
            q = (s * 3 + c) * MAIN
            a_ref[q : q + MAIN, columns] = jnp.where(here, wide, zero16)
            tail = jnp.where(i16 == jnp.full((16, LANES), c + 8 * s, BF16), wide, tail)
    a_ref[6 * MAIN :, columns] = jnp.where(row == jnp.full((16, LANES), MAIN, BF16), tail, zero16)


def factor_product(a_ref, b_ref, rows):
    return lax.dot_general(
        a_ref[:, : rows * LANES], b_ref[:, : rows * LANES], NT, preferred_element_type=F32
    )


def scatter(count, index_row, value_rows, a_ref, b_ref):
    def body(j, total):
        for k in range(CHUNK):
            r = j * CHUNK + k
            scatter_factors(index_row(r), value_rows(r), a_ref, b_ref, k)
        return total + factor_product(a_ref, b_ref, CHUNK)

    return lax.fori_loop(0, count // CHUNK, body, jnp.zeros((FACTOR_ROWS, LANES), F32))


def factor_sum(total):
    m = 3 * MAIN
    return jnp.concatenate([total[:m] + total[m : 2 * m], total[2 * m : 2 * m + 8] + total[2 * m + 8 :]], axis=0)


def pair_slots(owner_col, owner_row, cap):
    n = owner_row.shape[1]
    same = (owner_col == owner_row) & (iota((n, n), 0) < iota((n, n), 1))
    return jnp.sum(same.astype(F32), axis=0, keepdims=True)


def info_kernel(owner_col_ref, owner_row_ref, master_ref, normal_ref, out_ref, *, n_dom, cap):
    owner = owner_row_ref[...]
    n = owner.shape[1]
    rank = pair_slots(owner_col_ref[...], owner, cap)
    at = (iota((n_dom, n), 0) == owner).astype(F32)
    q = iota((4 * cap, n), 0)
    which = lax.div(q, cap)
    value = jnp.broadcast_to(master_ref[...].astype(F32), q.shape)
    for c in range(3):
        value = jnp.where(which == c, jnp.broadcast_to(normal_ref[c : c + 1, :], q.shape), value)
    value = jnp.where(lax.rem(q, cap).astype(F32) == rank, value, 0.0)
    out_ref[...] = dot_exact(at, value, NT)


def slave_side(owner_col_ref, owner_row_ref, slave_ref, normal_ref, patches, cap):
    owner = owner_row_ref[...]
    n = owner.shape[1]
    slot = owner.astype(F32) * cap + pair_slots(owner_col_ref[...], owner, cap)
    rho = iota((2 * SLOTS, n), 0)
    mine = (lax.div(rho, 2 * cap) * cap + lax.rem(rho, cap)).astype(F32)
    place = (mine == slot).astype(F32)
    hit = iota((patches, n), 0) == slave_ref[...]
    parts = [jnp.where(hit, jnp.broadcast_to(-normal_ref[c : c + 1, :], hit.shape), 0.0) for c in range(3)]
    parts.append(jnp.where(hit, -1.0, 0.0))
    return dot_exact(place, jnp.concatenate(parts, axis=0), NT)


def master_side(info, patches, n_dom, cap):
    rho = iota((2 * SLOTS, n_dom), 0)
    source = (lax.div(rho, 2 * cap) == iota((2 * SLOTS, n_dom), 1)).astype(F32)
    taken = dot_exact(source, info, NN)
    q = iota(taken.shape, 1)
    taken = jnp.where(lax.rem(q, cap) == lax.rem(iota(taken.shape, 0), cap), taken, 0.0)
    f = lax.div(iota((4 * cap, 3 * patches), 0), cap)
    normal = dot_exact(taken, (f == lax.div(iota(f.shape, 1), patches)).astype(F32), NN)
    master = dot_exact(taken, (f == 3).astype(F32), NN)
    column = lax.rem(iota(normal.shape, 1), patches).astype(F32)
    return jnp.where(jnp.abs(master - column) < 0.5, normal, 0.0)


def prepare_kernel(
    owner_col_ref, owner_row_ref, slave_ref, normal_ref, u_ref, v_ref, mass_ref, side_ref, fu_ref, fv_ref, fm_ref, *, patches, cap
):
    side_ref[...] = slave_side(owner_col_ref, owner_row_ref, slave_ref, normal_ref, patches, cap)
    to_field(u_ref, fu_ref)
    to_field(v_ref, fv_ref)
    fm_ref[...] = jnp.ones_like(fm_ref)
    for c in range(3):
        for h in range(MAIN + 1):
            r = field_row(c, h)
            fm_ref[r : r + 1, :] = mass_ref[0:1, h * LANES : (h + 1) * LANES]


def matrices_kernel(info_ref, side_ref, send_ref, keep_ref, *, masters, n_dom, cap):
    side = side_ref[...]
    owned = master_side(info_ref[...], masters, n_dom, cap)
    whole = jnp.concatenate([owned, side], axis=1)
    half = lax.rem(lax.div(iota(whole.shape, 0), cap), 2)
    right = jnp.where(iota(whole.shape, 1) < owned.shape[1], 0, 1)
    send_ref[...] = jnp.where(half == right, whole, 0.0)
    keep_ref[...] = jnp.where(half == right, 0.0, whole)


def pair_values(u_ref, snodes_ref, mnodes_ref, gap_ref, mortar_ref, x_ref, um_ref):
    masters, slaves = mnodes_ref.shape[0], snodes_ref.shape[0]

    def master_body(j, _):
        found = gather8(u_ref, mnodes_ref[pl.ds(j * 8, 8), :])
        for c in range(3):
            um_ref[pl.ds(c * masters + j * 8, 8), :] = found[c]
        return 0

    def slave_body(j, _):
        found = gather8(u_ref, snodes_ref[pl.ds(j * 8, 8), :])
        for c in range(3):
            x_ref[pl.ds(3 * masters + c * slaves + j * 8, 8), :] = found[c]
        return 0

    lax.fori_loop(0, masters // 8, master_body, 0, unroll=2)
    lax.fori_loop(0, slaves // 8, slave_body, 0, unroll=4)
    x_ref[: 3 * masters, :] = dot_exact(um_ref[...], mortar_ref[...], NT)
    x_ref[3 * (masters + slaves) :, :] = gap_ref[...]


def first_kernel(u_ref, snodes_ref, mnodes_ref, gap_ref, mortar_ref, send_ref, x_ref, out_ref, um_ref):
    pair_values(u_ref, snodes_ref, mnodes_ref, gap_ref, mortar_ref, x_ref, um_ref)
    out_ref[...] = dot_exact(send_ref[...], x_ref[...], NN)


def elastic_kernel(u_ref, conn_ref, modulus_ref, stiff_ref, keep_ref, x_ref, out_ref, kept_ref, ue_ref, idx_ref, a_ref, b_ref):
    kept_ref[...] = dot_exact(keep_ref[...], x_ref[...], NN)
    tiles = conn_ref.shape[1] // LANES

    def gather_body(j, _):
        columns = pl.ds(pl.multiple_of(j * LANES, LANES), LANES)
        index = conn_ref[:, columns]
        idx_ref[pl.ds(j * 8, 8), :] = index
        found = gather8(u_ref, index)
        for c in range(3):
            ue_ref[c * 8 : (c + 1) * 8, columns] = found[c]
        return 0

    lax.fori_loop(0, tiles, gather_body, 0, unroll=4)
    ue_ref[...] = dot_exact(stiff_ref[...], ue_ref[...], NN) * modulus_ref[...]

    def body(t, total):
        for k in range(CHUNK):
            j, a = t * (CHUNK // 8) + k // 8, k % 8
            columns = pl.ds(pl.multiple_of(j * LANES, LANES), LANES)
            values = [ue_ref[c * 8 + a : c * 8 + a + 1, columns] for c in range(3)]
            scatter_factors(idx_ref[pl.ds(t * CHUNK + k, 1), :], values, a_ref, b_ref, k)
        return total + factor_product(a_ref, b_ref, CHUNK)

    total = lax.fori_loop(0, tiles * 8 // CHUNK, body, jnp.zeros((FACTOR_ROWS, LANES), F32))
    out_ref[...] = factor_sum(total)


def contact_kernel(
    recv_ref, kept_ref, keep_ref, elastic_ref, snodes_ref, faces_ref, mortar_ref,
    local_ref, fa_ref, fb_ref, mf_ref, y_ref, a_ref, b_ref, *, masters,
):
    slaves = snodes_ref.shape[0]
    press = jnp.maximum(recv_ref[...] + kept_ref[...], 0.0)
    used = 3 * (masters + slaves)
    y_ref[...] = dot_exact(keep_ref[:, :used], press, TN)
    total = scatter(
        slaves,
        lambda r: snodes_ref[pl.ds(r, 1), :],
        lambda r: [y_ref[pl.ds(3 * masters + c * slaves + r, 1), :] for c in range(3)],
        a_ref,
        b_ref,
    )
    local_ref[...] = elastic_ref[...] + factor_sum(total)
    found = gather8(local_ref, faces_ref[...])
    for c in range(3):
        fa_ref[c, :, :] = found[c][:4]
        fb_ref[c, :, :] = found[c][4:]
    mf_ref[...] = dot_exact(y_ref[: 3 * masters, :], mortar_ref[...], NN)


def master_kernel(local_ref, mf_ref, mnodes_ref, out_ref, a_ref, b_ref):
    masters = mnodes_ref.shape[0]
    total = scatter(
        masters,
        lambda r: mnodes_ref[pl.ds(r, 1), :],
        lambda r: [mf_ref[pl.ds(c * masters + r, 1), :] for c in range(3)],
        a_ref,
        b_ref,
    )
    out_ref[...] = local_ref[...] + factor_sum(total)


def advance(negforce_ref, ra_ref, rb_ref, faces_ref, u_ref, v_ref, mass_ref, a_ref, b_ref):
    for k in range(8):
        r_ref = ra_ref if k < 4 else rb_ref
        values = [r_ref[c, k % 4 : k % 4 + 1, :] for c in range(3)]
        scatter_factors(faces_ref[k : k + 1, :], values, a_ref, b_ref, k)
    force = negforce_ref[...] + factor_sum(factor_product(a_ref, b_ref, 8))
    v = v_ref[...] - TIME_STEP * force / mass_ref[...]
    return u_ref[...] + TIME_STEP * v, v


def next_kernel(
    negforce_ref, ra_ref, rb_ref, faces_ref, u_ref, v_ref, mass_ref, snodes_ref, mnodes_ref, gap_ref, mortar_ref, send_ref,
    nu_ref, nv_ref, x_ref, out_ref, um_ref, a_ref, b_ref,
):
    u, v = advance(negforce_ref, ra_ref, rb_ref, faces_ref, u_ref, v_ref, mass_ref, a_ref, b_ref)
    nu_ref[...] = u
    nv_ref[...] = v
    pair_values(nu_ref, snodes_ref, mnodes_ref, gap_ref, mortar_ref, x_ref, um_ref)
    out_ref[...] = dot_exact(send_ref[...], x_ref[...], NN)


def last_kernel(negforce_ref, ra_ref, rb_ref, faces_ref, u_ref, v_ref, mass_ref, nu_ref, nv_ref, a_ref, b_ref):
    u, v = advance(negforce_ref, ra_ref, rb_ref, faces_ref, u_ref, v_ref, mass_ref, a_ref, b_ref)
    from_field(u, nu_ref)
    from_field(v, nv_ref)


def call(kernel, outs, args, scratch=(), us=1.0):
    vmem = pl.BlockSpec(memory_space=pltpu.VMEM)
    return pl.pallas_call(
        kernel,
        out_shape=[jax.ShapeDtypeStruct(s, F32) for s in outs],
        in_specs=[vmem] * len(args),
        out_specs=[vmem] * len(outs),
        scratch_shapes=list(scratch),
        compiler_params=pltpu.CompilerParams(vmem_limit_bytes=40 << 20),
        cost_estimate=pl.CostEstimate(flops=int(us * 1e9), bytes_accessed=int(us * 3e6), transcendentals=0),
    )(*args)


def shards(
    displacement,
    velocity,
    node_mass,
    connectivity,
    modulus,
    elem_stiffness,
    slave_nodes,
    slave_gap,
    master_nodes,
    pair_slave,
    pair_owner,
    pair_master,
    pair_normal,
    lower_face,
    upper_face,
    mortar,
):
    n_dom = lax.axis_size("dom")
    cap = SLOTS // n_dom
    slaves, masters = slave_nodes.shape[0], master_nodes.shape[0]
    elements = connectivity.shape[1]
    width = 3 * masters + 4 * slaves
    owner_row = pair_owner.reshape(1, -1)
    even = lax.axis_index("dom") % 2 == 0
    faces = jnp.concatenate(
        [jnp.where(even, upper_face, lower_face), jnp.where(even, lower_face, upper_face)]
    ).reshape(8, LANES)
    inside = [(i, i ^ 1) for i in range(n_dom)]
    across = [(i, i + 1) for i in range(1, n_dom - 1, 2)]
    across = across + [(j, i) for i, j in across]
    factors = (pltpu.VMEM((FACTOR_ROWS, CHUNK * LANES), BF16), pltpu.VMEM((LANES, CHUNK * LANES), BF16))

    (info,) = call(
        functools.partial(info_kernel, n_dom=n_dom, cap=cap),
        [(n_dom, 4 * cap)],
        (pair_owner, owner_row, pair_master.reshape(1, -1), pair_normal),
    )
    info = lax.all_to_all(info, "dom", 0, 0, tiled=True)
    side, u, v, mass = call(
        functools.partial(prepare_kernel, patches=slaves, cap=cap),
        [(2 * SLOTS, 4 * slaves)] + [(ROWS, LANES)] * 3,
        (pair_owner, owner_row, pair_slave.reshape(1, -1), pair_normal, displacement, velocity, node_mass.reshape(1, -1)),
    )
    send, keep = call(
        functools.partial(matrices_kernel, masters=masters, n_dom=n_dom, cap=cap), [(2 * SLOTS, width)] * 2, (info, side)
    )
    patch_scratch = pltpu.VMEM((3 * masters, LANES), F32)
    x, out = call(
        first_kernel,
        [(width, LANES), (2 * SLOTS, LANES)],
        (u, slave_nodes, master_nodes, slave_gap, mortar, send),
        [patch_scratch],
    )
    for step in range(STEPS):
        recv = lax.all_to_all(out.reshape(n_dom, 2 * cap, LANES), "dom", 0, 0).reshape(2 * SLOTS, LANES)
        elastic, kept = call(
            elastic_kernel,
            [(ROWS, LANES), (2 * SLOTS, LANES)],
            (u, connectivity, modulus.reshape(1, -1), elem_stiffness, keep, x),
            [pltpu.VMEM((24, elements), F32), pltpu.VMEM((8 * elements // LANES, LANES), jnp.int32), *factors],
            us=6.0,
        )
        local, fa, fb, mf = call(
            functools.partial(contact_kernel, masters=masters),
            [(ROWS, LANES), (3, 4, LANES), (3, 4, LANES), (3 * masters, LANES)],
            (recv, kept, keep, elastic, slave_nodes, faces, mortar),
            [pltpu.VMEM((3 * (masters + slaves), LANES), F32), *factors],
            us=3.0,
        )
        ra = lax.ppermute(fa, "dom", inside)
        rb = lax.ppermute(fb, "dom", across)
        (negforce,) = call(master_kernel, [(ROWS, LANES)], (local, mf, master_nodes), factors)
        state = (negforce, ra, rb, faces, u, v, mass)
        if step < STEPS - 1:
            u, v, x, out = call(
                next_kernel,
                [(ROWS, LANES), (ROWS, LANES), (width, LANES), (2 * SLOTS, LANES)],
                (*state, slave_nodes, master_nodes, slave_gap, mortar, send),
                [patch_scratch, *factors],
                us=3.0,
            )
        else:
            u, v = call(last_kernel, [displacement.shape, velocity.shape], state, factors)
    return (u, v)


def solution(mesh):
    return jax.shard_map(
        shards,
        mesh=mesh,
        in_specs=(
            P(None, ("groups", "dom")),
            P(None, ("groups", "dom")),
            P(("groups", "dom")),
            P(None, ("groups", "dom")),
            P(("groups", "dom")),
            P(),
            P(("groups", "dom"), None),
            P(("groups", "dom"), None),
            P(("groups", "dom"), None),
            P(("groups", "dom")),
            P(("groups", "dom"), None),
            P(("groups", "dom")),
            P(None, ("groups", "dom")),
            P(("groups", "dom")),
            P(("groups", "dom")),
            P(),
        ),
        out_specs=(P(None, ("groups", "dom")), P(None, ("groups", "dom"))),
        check_vma=False,
    )
```

```python
import functools

import jax
import jax.numpy as jnp
from jax import lax
from jax.experimental import pallas as pl
from jax.experimental.pallas import tpu as pltpu
from jax.sharding import PartitionSpec as P

LANES = 128
STEPS = 3
TIME_STEP = 0.1
SLOTS = 256
GROUP = 4

F32 = jnp.float32
BF16 = jnp.bfloat16
HIGH = lax.Precision.HIGHEST
NN = (((1,), (0,)), ((), ()))
NT = (((1,), (1,)), ((), ()))
TN = (((0,), (0,)), ((), ()))

MAIN = 16
ROWS = 56
FACTOR_ROWS = 112


def dot_exact(a, b, dims):
    return lax.dot_general(a, b, dims, precision=HIGH, preferred_element_type=F32)


def iota(shape, dim):
    return lax.broadcasted_iota(jnp.int32, shape, dim)


def field_row(c, h):
    return c * MAIN + h if h < MAIN else 3 * MAIN + c


def to_field(flat_ref, field_ref):
    field_ref[...] = jnp.zeros_like(field_ref)
    for c in range(3):
        for h in range(MAIN + 1):
            r = field_row(c, h)
            field_ref[r : r + 1, :] = flat_ref[c : c + 1, h * LANES : (h + 1) * LANES]


def from_field(field, flat_ref):
    for c in range(3):
        for h in range(MAIN + 1):
            r = field_row(c, h)
            flat_ref[c : c + 1, h * LANES : (h + 1) * LANES] = field[r : r + 1, :]


def gather8(field_ref, index):
    lane = index & (LANES - 1)
    row = index >> 7
    bits = [(row & (1 << q)) != 0 for q in range(4)]
    last = row >= MAIN
    found = []
    for c in range(3):
        values = []
        for h in range(MAIN + 1):
            r = field_row(c, h)
            table = jnp.broadcast_to(field_ref[r : r + 1, :], (8, LANES))
            values.append(jnp.take_along_axis(table, lane, axis=1, mode="promise_in_bounds"))
        tail = values.pop()
        for bit in bits:
            values = [jnp.where(bit, values[i + 1], values[i]) for i in range(0, len(values), 2)]
        found.append(jnp.where(last, tail, values[0]))
    return found


def value_factor(index, values):
    i16 = iota((MAIN, LANES), 0).astype(F32).astype(BF16)
    row = jnp.broadcast_to((index >> 7).astype(F32), (MAIN, LANES)).astype(BF16)
    zero = jnp.zeros((MAIN, LANES), BF16)
    here = i16 == row
    tail, out = zero, []
    for s in range(2):
        for c in range(3):
            high = values[c].astype(BF16).astype(F32)
            part = values[c] - high if s else high
            wide = jnp.broadcast_to(part, (MAIN, LANES)).astype(BF16)
            out.append(jnp.where(here, wide, zero))
            tail = jnp.where(i16 == jnp.full(i16.shape, c + 8 * s, BF16), wide, tail)
    out.append(jnp.where(row == jnp.full(row.shape, MAIN, BF16), tail, zero))
    return jnp.concatenate(out, axis=0)


def lane_factor(index):
    i128 = iota((LANES, LANES), 0).astype(F32).astype(BF16)
    lane = jnp.broadcast_to((index & (LANES - 1)).astype(F32), (LANES, LANES)).astype(BF16)
    return jnp.where(i128 == lane, jnp.ones((LANES, LANES), BF16), jnp.zeros((LANES, LANES), BF16))


def scatter(rows, total=None):
    for j in range(0, len(rows), GROUP):
        group = rows[j : j + GROUP]
        a = jnp.concatenate([value_factor(index, values) for index, values in group], axis=1)
        b = jnp.concatenate([lane_factor(index) for index, _ in group], axis=1)
        part = lax.dot_general(a, b, NT, preferred_element_type=F32)
        total = part if total is None else total + part
    return total


def factor_sum(total):
    m = 3 * MAIN
    return jnp.concatenate([total[:m] + total[m : 2 * m], total[2 * m : 2 * m + 8] + total[2 * m + 8 :]], axis=0)


def two_parts(x):
    high = x.astype(BF16)
    return high, (x - high.astype(F32)).astype(BF16)


def as_left(x, axis=1):
    high, low = two_parts(x)
    return jnp.concatenate([high, high, low], axis=axis)


def as_right(x, axis=0):
    high, low = two_parts(x)
    return jnp.concatenate([high, low, high], axis=axis)


def product(a, b):
    return lax.dot_general(a, b, NN, preferred_element_type=F32)


def take_slots(block_ref, half, cap):
    n_dom = block_ref.shape[0]
    rows = slice(half * cap, (half + 1) * cap)
    if cap % 8 == 0:
        return block_ref[:, rows, :].reshape(n_dom * cap, LANES)
    return jnp.concatenate([block_ref[o, rows, :] for o in range(n_dom)], axis=0)


def put_slots(block_ref, half, cap, value):
    n_dom = block_ref.shape[0]
    rows = slice(half * cap, (half + 1) * cap)
    if cap % 8 == 0:
        block_ref[:, rows, :] = value.reshape(n_dom, cap, LANES)
    else:
        for o in range(n_dom):
            block_ref[o, rows, :] = value[o * cap : (o + 1) * cap]


def ranks(owner):
    n = owner.shape[1]
    across = jnp.broadcast_to(owner.astype(F32), (n, n))
    same = (across.T == across) & (iota((n, n), 0) < iota((n, n), 1))
    return jnp.sum(same.astype(F32), axis=0, keepdims=True)


def info_kernel(owner_ref, master_ref, normal_ref, out_ref, *, n_dom, cap):
    owner = owner_ref[...]
    n = owner.shape[1]
    at = (iota((n_dom, n), 0) == owner).astype(F32)
    q = iota((4 * cap, n), 0)
    which = lax.div(q, cap)
    value = jnp.broadcast_to(master_ref[...].astype(F32), q.shape)
    for c in range(3):
        value = jnp.where(which == c, jnp.broadcast_to(normal_ref[c : c + 1, :], q.shape), value)
    value = jnp.where(lax.rem(q, cap).astype(F32) == ranks(owner), value, 0.0)
    out_ref[...] = dot_exact(at, value, NT)


def gathered(field_ref, nodes_ref):
    blocks = [gather8(field_ref, nodes_ref[j : j + 8, :]) for j in range(0, nodes_ref.shape[0], 8)]
    return [jnp.concatenate([b[c] for b in blocks], axis=0) for c in range(3)]


def pair_values(u_ref, snodes_ref, mnodes_ref, gap_ref, mortar_t_ref, slave_ref):
    um = jnp.concatenate(gathered(u_ref, mnodes_ref), axis=0)
    mapped = product(as_right(um, 1), mortar_t_ref[...])
    us = jnp.concatenate([*gathered(u_ref, snodes_ref), gap_ref[...]], axis=0)
    return mapped, product(slave_ref[...], as_right(us))


def prepare_kernel(
    owner_ref, pair_slave_ref, normal_ref, u_ref, v_ref, mass_ref, snodes_ref, mnodes_ref, gap_ref, mortar_ref,
    slave_ref, slave_t_ref, mortar_left_ref, mortar_t_ref, fu_ref, fv_ref, fm_ref, mapped_ref, neg_gap_ref, *, cap,
):
    owner, patches = owner_ref[...], snodes_ref.shape[0]
    n = owner.shape[1]
    slot = owner.astype(F32) * cap + ranks(owner)
    place = (iota((SLOTS, n), 0).astype(F32) == slot).astype(F32)
    hit = iota((patches, n), 0) == pair_slave_ref[...]
    parts = [jnp.where(hit, jnp.broadcast_to(-normal_ref[c : c + 1, :], hit.shape), 0.0) for c in range(3)]
    slave_t_ref[...] = as_left(dot_exact(jnp.concatenate(parts, axis=0), place, NT))
    parts.append(jnp.where(hit, -1.0, 0.0))
    slave_ref[...] = as_left(dot_exact(place, jnp.concatenate(parts, axis=0), NT))
    mortar = mortar_ref[...]
    mortar_left_ref[...] = as_left(mortar, 0)
    mortar_t_ref[...] = as_left(mortar.T, 0)
    to_field(u_ref, fu_ref)
    to_field(v_ref, fv_ref)
    fm_ref[...] = jnp.ones_like(fm_ref)
    for c in range(3):
        for h in range(MAIN + 1):
            r = field_row(c, h)
            fm_ref[r : r + 1, :] = mass_ref[0:1, h * LANES : (h + 1) * LANES]
    mapped, neg_gap = pair_values(fu_ref, snodes_ref, mnodes_ref, gap_ref, mortar_t_ref, slave_ref)
    mapped_ref[...] = mapped
    neg_gap_ref[...] = neg_gap


def first_kernel(info_ref, mapped_ref, neg_gap_ref, out_ref, master_ref, *, cap):
    n_dom, masters = info_ref.shape[0], mapped_ref.shape[0] // 3
    taken = jnp.concatenate([jnp.broadcast_to(info_ref[o : o + 1, :], (cap, 4 * cap)) for o in range(n_dom)], axis=0)
    mine = lax.rem(iota(taken.shape, 1), cap) == lax.rem(iota(taken.shape, 0), cap)
    f = lax.div(iota((4 * cap, 2 * LANES), 0), cap)
    column = iota(f.shape, 1)
    spread = ((f == lax.div(column, masters)) & (column < LANES)) | ((f == 3) & (column >= LANES))
    both = dot_exact(jnp.where(mine, taken, 0.0), spread.astype(F32), NN)
    number = lax.rem(iota((SLOTS, LANES), 1), masters).astype(F32)
    owned = jnp.where(jnp.abs(both[:, LANES:] - number) < 0.5, both[:, :LANES], 0.0)[:, : 3 * masters]
    master_ref[...] = owned
    put_slots(out_ref, 0, cap, product(as_left(owned), as_right(mapped_ref[...])))
    put_slots(out_ref, 1, cap, neg_gap_ref[...])


def turn_kernel(owned_ref, master_ref, master_t_ref):
    owned = owned_ref[...]
    master_ref[...] = as_left(owned)
    n = owned.shape[1]
    eye = (iota((n, n), 0) == iota((n, n), 1)).astype(F32)
    master_t_ref[...] = as_left(dot_exact(eye, owned, NT))


def elastic_kernel(u_ref, conn_ref, modulus_ref, stiff_ref, out_ref, ue_ref):
    tiles = conn_ref.shape[1] // LANES

    def gather_body(j, _):
        columns = pl.ds(pl.multiple_of(j * LANES, LANES), LANES)
        found = gather8(u_ref, conn_ref[:, columns])
        for c in range(3):
            ue_ref[c * 8 : (c + 1) * 8, columns] = found[c]
        return 0

    lax.fori_loop(0, tiles, gather_body, 0, unroll=4)
    ue_ref[...] = dot_exact(stiff_ref[...], ue_ref[...], NN) * modulus_ref[...]

    def body(j, total):
        columns = pl.ds(pl.multiple_of(j * LANES, LANES), LANES)
        rows = []
        for a in range(8):
            rows.append((conn_ref[a : a + 1, columns], [ue_ref[c * 8 + a : c * 8 + a + 1, columns] for c in range(3)]))
        return scatter(rows, total)

    total = lax.fori_loop(0, tiles, body, jnp.zeros((FACTOR_ROWS, LANES), F32), unroll=2)
    out_ref[...] = factor_sum(total)


def patch_rows(nodes_ref, values_ref):
    patches = nodes_ref.shape[0]
    return [
        (nodes_ref[r : r + 1, :], [values_ref[c * patches + r : c * patches + r + 1, :] for c in range(3)])
        for r in range(patches)
    ]


def contact_kernel(
    recv_ref, sent_ref, slave_t_ref, elastic_ref, snodes_ref, faces_ref, local_ref, fa_ref, fb_ref, y_ref, *, cap
):
    press = jnp.maximum(take_slots(recv_ref, 0, cap) + take_slots(sent_ref, 1, cap), 0.0)
    y_ref[...] = product(slave_t_ref[...], as_right(press))
    local_ref[...] = elastic_ref[...] + factor_sum(scatter(patch_rows(snodes_ref, y_ref)))
    found = gather8(local_ref, faces_ref[...])
    for c in range(3):
        fa_ref[c, :, :] = found[c][:4]
        fb_ref[c, :, :] = found[c][4:]


def master_kernel(recv_ref, sent_ref, master_t_ref, mortar_ref, local_ref, mnodes_ref, out_ref, y_ref, *, cap):
    press = jnp.maximum(take_slots(sent_ref, 0, cap) + take_slots(recv_ref, 1, cap), 0.0)
    summed = product(master_t_ref[...], as_right(press))
    y_ref[...] = product(as_right(summed, 1), mortar_ref[...])
    out_ref[...] = local_ref[...] + factor_sum(scatter(patch_rows(mnodes_ref, y_ref)))


def advance(negforce_ref, ra_ref, rb_ref, faces_ref, u_ref, v_ref, mass_ref):
    rows = []
    for k in range(8):
        r_ref = ra_ref if k < 4 else rb_ref
        rows.append((faces_ref[k : k + 1, :], [r_ref[c, k % 4 : k % 4 + 1, :] for c in range(3)]))
    force = negforce_ref[...] + factor_sum(scatter(rows))
    v = v_ref[...] - TIME_STEP * force / mass_ref[...]
    return u_ref[...] + TIME_STEP * v, v


def next_kernel(
    negforce_ref, ra_ref, rb_ref, faces_ref, u_ref, v_ref, mass_ref, snodes_ref, mnodes_ref, gap_ref, mortar_t_ref, slave_ref,
    master_ref, nu_ref, nv_ref, out_ref, *, cap,
):
    u, v = advance(negforce_ref, ra_ref, rb_ref, faces_ref, u_ref, v_ref, mass_ref)
    nu_ref[...] = u
    nv_ref[...] = v
    mapped, neg_gap = pair_values(nu_ref, snodes_ref, mnodes_ref, gap_ref, mortar_t_ref, slave_ref)
    put_slots(out_ref, 1, cap, neg_gap)
    put_slots(out_ref, 0, cap, product(master_ref[...], as_right(mapped)))


def last_kernel(negforce_ref, ra_ref, rb_ref, faces_ref, u_ref, v_ref, mass_ref, nu_ref, nv_ref):
    u, v = advance(negforce_ref, ra_ref, rb_ref, faces_ref, u_ref, v_ref, mass_ref)
    from_field(u, nu_ref)
    from_field(v, nv_ref)


def call(kernel, outs, args, scratch=(), us=1.0):
    vmem = pl.BlockSpec(memory_space=pltpu.VMEM)
    return pl.pallas_call(
        kernel,
        out_shape=outs,
        in_specs=[vmem] * len(args),
        out_specs=[vmem] * len(outs),
        scratch_shapes=list(scratch),
        compiler_params=pltpu.CompilerParams(vmem_limit_bytes=40 << 20),
        cost_estimate=pl.CostEstimate(flops=int(us * 1e9), bytes_accessed=int(us * 3e6), transcendentals=0),
    )(*args)


def shards(
    displacement,
    velocity,
    node_mass,
    connectivity,
    modulus,
    elem_stiffness,
    slave_nodes,
    slave_gap,
    master_nodes,
    pair_slave,
    pair_owner,
    pair_master,
    pair_normal,
    lower_face,
    upper_face,
    mortar,
):
    n_dom = lax.axis_size("dom")
    cap = SLOTS // n_dom
    slaves, masters = slave_nodes.shape[0], master_nodes.shape[0]
    f32 = lambda *shape: jax.ShapeDtypeStruct(shape, F32)
    bf16 = lambda *shape: jax.ShapeDtypeStruct(shape, BF16)
    field = f32(ROWS, LANES)
    owner = pair_owner.reshape(1, -1)
    even = lax.axis_index("dom") % 2 == 0
    faces = jnp.concatenate(
        [jnp.where(even, upper_face, lower_face), jnp.where(even, lower_face, upper_face)]
    ).reshape(8, LANES)
    inside = [(i, i ^ 1) for i in range(n_dom)]
    across = [(i, i + 1) for i in range(1, n_dom - 1, 2)]
    across = across + [(j, i) for i, j in across]

    (info,) = call(
        functools.partial(info_kernel, n_dom=n_dom, cap=cap),
        [f32(n_dom, 4 * cap)],
        (owner, pair_master.reshape(1, -1), pair_normal),
    )
    info = lax.all_to_all(info, "dom", 0, 0, tiled=True)
    slave, slave_t, mortar_left, mortar_t, u, v, mass, mapped, neg_gap = call(
        functools.partial(prepare_kernel, cap=cap),
        [
            bf16(SLOTS, 12 * slaves),
            bf16(3 * slaves, 3 * SLOTS),
            bf16(3 * LANES, LANES),
            bf16(3 * LANES, LANES),
            field,
            field,
            field,
            f32(3 * masters, LANES),
            f32(SLOTS, LANES),
        ],
        (
            owner,
            pair_slave.reshape(1, -1),
            pair_normal,
            displacement,
            velocity,
            node_mass.reshape(1, -1),
            slave_nodes,
            master_nodes,
            slave_gap,
            mortar,
        ),
        us=3.0,
    )
    blocks = f32(n_dom, 2 * cap, LANES)
    out, owned = call(functools.partial(first_kernel, cap=cap), [blocks, f32(SLOTS, 3 * masters)], (info, mapped, neg_gap))
    for step in range(STEPS):
        recv = lax.all_to_all(out, "dom", 0, 0)
        (elastic,) = call(
            elastic_kernel,
            [field],
            (u, connectivity, modulus.reshape(1, -1), elem_stiffness),
            [pltpu.VMEM((24, connectivity.shape[1]), F32)],
            us=5.0,
        )
        if step == 0:
            master, master_t = call(turn_kernel, [bf16(SLOTS, 9 * masters), bf16(3 * masters, 3 * SLOTS)], (owned,))
        local, fa, fb = call(
            functools.partial(contact_kernel, cap=cap),
            [field, f32(3, 4, LANES), f32(3, 4, LANES)],
            (recv, out, slave_t, elastic, slave_nodes, faces),
            [pltpu.VMEM((3 * slaves, LANES), F32)],
            us=2.0,
        )
        ra = lax.ppermute(fa, "dom", inside)
        rb = lax.ppermute(fb, "dom", across)
        (negforce,) = call(
            functools.partial(master_kernel, cap=cap),
            [field],
            (recv, out, master_t, mortar_left, local, master_nodes),
            [pltpu.VMEM((3 * masters, LANES), F32)],
        )
        state = (negforce, ra, rb, faces, u, v, mass)
        if step < STEPS - 1:
            u, v, out = call(
                functools.partial(next_kernel, cap=cap),
                [field, field, blocks],
                (*state, slave_nodes, master_nodes, slave_gap, mortar_t, slave, master),
                us=2.0,
            )
        else:
            outs = [f32(*displacement.shape), f32(*velocity.shape)]
            u, v = call(last_kernel, outs, state)
    return (u, v)


def solution(mesh):
    return jax.shard_map(
        shards,
        mesh=mesh,
        in_specs=(
            P(None, ("groups", "dom")),
            P(None, ("groups", "dom")),
            P(("groups", "dom")),
            P(None, ("groups", "dom")),
            P(("groups", "dom")),
            P(),
            P(("groups", "dom"), None),
            P(("groups", "dom"), None),
            P(("groups", "dom"), None),
            P(("groups", "dom")),
            P(("groups", "dom"), None),
            P(("groups", "dom")),
            P(None, ("groups", "dom")),
            P(("groups", "dom")),
            P(("groups", "dom")),
            P(),
        ),
        out_specs=(P(None, ("groups", "dom")), P(None, ("groups", "dom"))),
        check_vma=False,
    )
```

```python
import functools

import jax
import jax.numpy as jnp
from jax import lax
from jax.experimental import pallas as pl
from jax.experimental.pallas import tpu as pltpu
from jax.sharding import PartitionSpec as P

LANES = 128
STEPS = 3
TIME_STEP = 0.1
SLOTS = 256
GROUP = 4

F32 = jnp.float32
BF16 = jnp.bfloat16
HIGH = lax.Precision.HIGHEST
NN = (((1,), (0,)), ((), ()))
NT = (((1,), (1,)), ((), ()))
TN = (((0,), (0,)), ((), ()))

MAIN = 16
ROWS = 56
FACTOR_ROWS = 112


def dot_exact(a, b, dims):
    return lax.dot_general(a, b, dims, precision=HIGH, preferred_element_type=F32)


def iota(shape, dim):
    return lax.broadcasted_iota(jnp.int32, shape, dim)


def field_row(c, h):
    return c * MAIN + h if h < MAIN else 3 * MAIN + c


def to_field(flat_ref, field_ref):
    field_ref[...] = jnp.zeros_like(field_ref)
    for c in range(3):
        for h in range(MAIN + 1):
            r = field_row(c, h)
            field_ref[r : r + 1, :] = flat_ref[c : c + 1, h * LANES : (h + 1) * LANES]


def from_field(field, flat_ref):
    for c in range(3):
        for h in range(MAIN + 1):
            r = field_row(c, h)
            flat_ref[c : c + 1, h * LANES : (h + 1) * LANES] = field[r : r + 1, :]


def gather8(field_ref, index):
    lane = index & (LANES - 1)
    row = index >> 7
    bits = [(row & (1 << q)) != 0 for q in range(4)]
    last = row >= MAIN
    found = []
    for c in range(3):
        values = []
        for h in range(MAIN + 1):
            r = field_row(c, h)
            table = jnp.broadcast_to(field_ref[r : r + 1, :], (8, LANES))
            values.append(jnp.take_along_axis(table, lane, axis=1, mode="promise_in_bounds"))
        tail = values.pop()
        for bit in bits:
            values = [jnp.where(bit, values[i + 1], values[i]) for i in range(0, len(values), 2)]
        found.append(jnp.where(last, tail, values[0]))
    return found


def value_factor(index, values):
    i16 = iota((MAIN, LANES), 0).astype(F32).astype(BF16)
    row = jnp.broadcast_to((index >> 7).astype(F32), (MAIN, LANES)).astype(BF16)
    zero = jnp.zeros((MAIN, LANES), BF16)
    here = i16 == row
    tail, out = zero, []
    for s in range(2):
        for c in range(3):
            high = values[c].astype(BF16).astype(F32)
            part = values[c] - high if s else high
            wide = jnp.broadcast_to(part, (MAIN, LANES)).astype(BF16)
            out.append(jnp.where(here, wide, zero))
            tail = jnp.where(i16 == jnp.full(i16.shape, c + 8 * s, BF16), wide, tail)
    out.append(jnp.where(row == jnp.full(row.shape, MAIN, BF16), tail, zero))
    return jnp.concatenate(out, axis=0)


def lane_factor(index):
    i128 = iota((LANES, LANES), 0).astype(F32).astype(BF16)
    lane = jnp.broadcast_to((index & (LANES - 1)).astype(F32), (LANES, LANES)).astype(BF16)
    return jnp.where(i128 == lane, jnp.ones((LANES, LANES), BF16), jnp.zeros((LANES, LANES), BF16))


def scatter(rows, total=None):
    for j in range(0, len(rows), GROUP):
        group = rows[j : j + GROUP]
        a = jnp.concatenate([value_factor(index, values) for index, values in group], axis=1)
        b = jnp.concatenate([lane_factor(index) for index, _ in group], axis=1)
        part = lax.dot_general(a, b, NT, preferred_element_type=F32)
        total = part if total is None else total + part
    return total


def factor_sum(total):
    m = 3 * MAIN
    return jnp.concatenate([total[:m] + total[m : 2 * m], total[2 * m : 2 * m + 8] + total[2 * m + 8 :]], axis=0)


def two_parts(x):
    high = x.astype(BF16)
    return high, (x - high.astype(F32)).astype(BF16)


def as_left(x, axis=1):
    high, low = two_parts(x)
    return jnp.concatenate([high, high, low], axis=axis)


def as_right(x, axis=0):
    high, low = two_parts(x)
    return jnp.concatenate([high, low, high], axis=axis)


def product(a, b):
    return lax.dot_general(a, b, NN, preferred_element_type=F32)


def take_slots(block_ref, half, cap):
    n_dom = block_ref.shape[0]
    rows = slice(half * cap, (half + 1) * cap)
    if cap % 8 == 0:
        return block_ref[:, rows, :].reshape(n_dom * cap, LANES)
    return jnp.concatenate([block_ref[o, rows, :] for o in range(n_dom)], axis=0)


def put_slots(block_ref, half, cap, value):
    n_dom = block_ref.shape[0]
    rows = slice(half * cap, (half + 1) * cap)
    if cap % 8 == 0:
        block_ref[:, rows, :] = value.reshape(n_dom, cap, LANES)
    else:
        for o in range(n_dom):
            block_ref[o, rows, :] = value[o * cap : (o + 1) * cap]


def ranks(owner, n_dom):
    n = owner.shape[1]
    at = (iota((n_dom, n), 0) == owner).astype(F32)
    before = (iota((n, n), 0) < iota((n, n), 1)).astype(F32)
    counts = lax.dot_general(at.astype(BF16), before.astype(BF16), NN, preferred_element_type=F32)
    return jnp.sum(at * counts, axis=0, keepdims=True), at


def info_kernel(owner_ref, master_ref, normal_ref, out_ref, *, n_dom, cap):
    rank, at = ranks(owner_ref[...], n_dom)
    q = iota((4 * cap, owner_ref.shape[1]), 0)
    which = lax.div(q, cap)
    value = jnp.broadcast_to(master_ref[...].astype(F32), q.shape)
    for c in range(3):
        value = jnp.where(which == c, jnp.broadcast_to(normal_ref[c : c + 1, :], q.shape), value)
    value = jnp.where(lax.rem(q, cap).astype(F32) == rank, value, 0.0)
    out_ref[...] = dot_exact(at, value, NT)


def gathered(field_ref, nodes_ref):
    blocks = [gather8(field_ref, nodes_ref[j : j + 8, :]) for j in range(0, nodes_ref.shape[0], 8)]
    return [jnp.concatenate([b[c] for b in blocks], axis=0) for c in range(3)]


def pair_values(u_ref, snodes_ref, mnodes_ref, gap_ref, mortar_t_ref, slave_ref):
    um = jnp.concatenate(gathered(u_ref, mnodes_ref), axis=0)
    mapped = product(as_right(um, 1), mortar_t_ref[...])
    us = jnp.concatenate([*gathered(u_ref, snodes_ref), gap_ref[...]], axis=0)
    return mapped, product(slave_ref[...], as_right(us))


def prepare_kernel(
    owner_ref, pair_slave_ref, normal_ref, u_ref, v_ref, mass_ref, snodes_ref, mnodes_ref, gap_ref, mortar_ref,
    slave_ref, slave_t_ref, mortar_left_ref, mortar_t_ref, fu_ref, fv_ref, fm_ref, mapped_ref, neg_gap_ref, *, n_dom, cap,
):
    owner, patches = owner_ref[...], snodes_ref.shape[0]
    n = owner.shape[1]
    slot = owner.astype(F32) * cap + ranks(owner, n_dom)[0]
    place = (iota((SLOTS, n), 0).astype(F32) == slot).astype(F32)
    hit = iota((patches, n), 0) == pair_slave_ref[...]
    parts = [jnp.where(hit, jnp.broadcast_to(-normal_ref[c : c + 1, :], hit.shape), 0.0) for c in range(3)]
    slave_t_ref[...] = as_left(dot_exact(jnp.concatenate(parts, axis=0), place, NT))
    parts.append(jnp.where(hit, -1.0, 0.0))
    slave_ref[...] = as_left(dot_exact(place, jnp.concatenate(parts, axis=0), NT))
    mortar = mortar_ref[...]
    mortar_left_ref[...] = as_left(mortar, 0)
    mortar_t_ref[...] = as_left(mortar.T, 0)
    to_field(u_ref, fu_ref)
    to_field(v_ref, fv_ref)
    fm_ref[...] = jnp.ones_like(fm_ref)
    for c in range(3):
        for h in range(MAIN + 1):
            r = field_row(c, h)
            fm_ref[r : r + 1, :] = mass_ref[0:1, h * LANES : (h + 1) * LANES]
    mapped, neg_gap = pair_values(fu_ref, snodes_ref, mnodes_ref, gap_ref, mortar_t_ref, slave_ref)
    mapped_ref[...] = mapped
    neg_gap_ref[...] = neg_gap


def first_kernel(info_ref, mapped_ref, neg_gap_ref, out_ref, m_ref, master_ref, *, cap):
    n_dom, masters = info_ref.shape[0], mapped_ref.shape[0] // 3
    taken = jnp.concatenate([jnp.broadcast_to(info_ref[o : o + 1, :], (cap, 4 * cap)) for o in range(n_dom)], axis=0)
    mine = lax.rem(iota(taken.shape, 1), cap) == lax.rem(iota(taken.shape, 0), cap)
    f = lax.div(iota((4 * cap, 2 * LANES), 0), cap)
    column = iota(f.shape, 1)
    spread = ((f == lax.div(column, masters)) & (column < LANES)) | ((f == 3) & (column >= LANES))
    both = dot_exact(jnp.where(mine, taken, 0.0), spread.astype(F32), NN)
    number = lax.rem(iota((SLOTS, LANES), 1), masters).astype(F32)
    owned = jnp.where(jnp.abs(both[:, LANES:] - number) < 0.5, both[:, :LANES], 0.0)[:, : 3 * masters]
    master_ref[...] = owned
    put_slots(out_ref, 1, cap, neg_gap_ref[...])
    m_ref[...] = product(as_left(owned), as_right(mapped_ref[...]))
    put_slots(out_ref, 0, cap, m_ref[...])


def turn_kernel(owned_ref, master_ref, master_t_ref):
    owned = owned_ref[...]
    master_ref[...] = as_left(owned)
    n = owned.shape[1]
    eye = (iota((n, n), 0) == iota((n, n), 1)).astype(F32)
    master_t_ref[...] = as_left(dot_exact(eye, owned, NT))


def elastic_kernel(u_ref, conn_ref, modulus_ref, stiff_ref, out_ref, ue_ref):
    tiles = conn_ref.shape[1] // LANES

    def gather_body(j, _):
        columns = pl.ds(pl.multiple_of(j * LANES, LANES), LANES)
        found = gather8(u_ref, conn_ref[:, columns])
        for c in range(3):
            ue_ref[c * 8 : (c + 1) * 8, columns] = found[c]
        return 0

    lax.fori_loop(0, tiles, gather_body, 0, unroll=4)
    ue_ref[...] = dot_exact(stiff_ref[...], ue_ref[...], NN) * modulus_ref[...]

    def body(j, total):
        columns = pl.ds(pl.multiple_of(j * LANES, LANES), LANES)
        rows = []
        for a in range(8):
            rows.append((conn_ref[a : a + 1, columns], [ue_ref[c * 8 + a : c * 8 + a + 1, columns] for c in range(3)]))
        return scatter(rows, total)

    total = lax.fori_loop(0, tiles, body, jnp.zeros((FACTOR_ROWS, LANES), F32), unroll=2)
    out_ref[...] = factor_sum(total)


def patch_rows(nodes_ref, values_ref):
    patches = nodes_ref.shape[0]
    return [
        (nodes_ref[r : r + 1, :], [values_ref[c * patches + r : c * patches + r + 1, :] for c in range(3)])
        for r in range(patches)
    ]


def contact_kernel(
    recv_ref, neg_gap_ref, slave_t_ref, elastic_ref, snodes_ref, faces_ref, local_ref, fa_ref, fb_ref, y_ref, *, cap
):
    press = jnp.maximum(take_slots(recv_ref, 0, cap) + neg_gap_ref[...], 0.0)
    y_ref[...] = product(slave_t_ref[...], as_right(press))
    local_ref[...] = elastic_ref[...] + factor_sum(scatter(patch_rows(snodes_ref, y_ref)))
    found = gather8(local_ref, faces_ref[...])
    for c in range(3):
        fa_ref[c, :, :] = found[c][:4]
        fb_ref[c, :, :] = found[c][4:]


def master_kernel(recv_ref, m_ref, master_t_ref, mortar_ref, local_ref, mnodes_ref, out_ref, y_ref, *, cap):
    press = jnp.maximum(m_ref[...] + take_slots(recv_ref, 1, cap), 0.0)
    summed = product(master_t_ref[...], as_right(press))
    y_ref[...] = product(as_right(summed, 1), mortar_ref[...])
    out_ref[...] = local_ref[...] + factor_sum(scatter(patch_rows(mnodes_ref, y_ref)))


def advance(negforce_ref, ra_ref, rb_ref, faces_ref, u_ref, v_ref, mass_ref):
    rows = []
    for k in range(8):
        r_ref = ra_ref if k < 4 else rb_ref
        rows.append((faces_ref[k : k + 1, :], [r_ref[c, k % 4 : k % 4 + 1, :] for c in range(3)]))
    force = negforce_ref[...] + factor_sum(scatter(rows))
    v = v_ref[...] - TIME_STEP * force / mass_ref[...]
    return u_ref[...] + TIME_STEP * v, v


def next_kernel(
    negforce_ref, ra_ref, rb_ref, faces_ref, u_ref, v_ref, mass_ref, snodes_ref, mnodes_ref, gap_ref, mortar_t_ref, slave_ref,
    master_ref, nu_ref, nv_ref, out_ref, m_ref, neg_gap_ref, *, cap,
):
    u, v = advance(negforce_ref, ra_ref, rb_ref, faces_ref, u_ref, v_ref, mass_ref)
    nu_ref[...] = u
    nv_ref[...] = v
    mapped, neg_gap = pair_values(nu_ref, snodes_ref, mnodes_ref, gap_ref, mortar_t_ref, slave_ref)
    neg_gap_ref[...] = neg_gap
    put_slots(out_ref, 1, cap, neg_gap)
    m_ref[...] = product(master_ref[...], as_right(mapped))
    put_slots(out_ref, 0, cap, m_ref[...])


def last_kernel(negforce_ref, ra_ref, rb_ref, faces_ref, u_ref, v_ref, mass_ref, nu_ref, nv_ref):
    u, v = advance(negforce_ref, ra_ref, rb_ref, faces_ref, u_ref, v_ref, mass_ref)
    from_field(u, nu_ref)
    from_field(v, nv_ref)


def call(kernel, outs, args, scratch=(), us=1.0):
    vmem = pl.BlockSpec(memory_space=pltpu.VMEM)
    return pl.pallas_call(
        kernel,
        out_shape=outs,
        in_specs=[vmem] * len(args),
        out_specs=[vmem] * len(outs),
        scratch_shapes=list(scratch),
        compiler_params=pltpu.CompilerParams(vmem_limit_bytes=40 << 20),
        cost_estimate=pl.CostEstimate(flops=int(us * 1e9), bytes_accessed=int(us * 3e6), transcendentals=0),
    )(*args)


def shards(
    displacement,
    velocity,
    node_mass,
    connectivity,
    modulus,
    elem_stiffness,
    slave_nodes,
    slave_gap,
    master_nodes,
    pair_slave,
    pair_owner,
    pair_master,
    pair_normal,
    lower_face,
    upper_face,
    mortar,
):
    n_dom = lax.axis_size("dom")
    cap = SLOTS // n_dom
    slaves, masters = slave_nodes.shape[0], master_nodes.shape[0]
    f32 = lambda *shape: jax.ShapeDtypeStruct(shape, F32)
    bf16 = lambda *shape: jax.ShapeDtypeStruct(shape, BF16)
    field = f32(ROWS, LANES)
    owner = pair_owner.reshape(1, -1)
    even = lax.axis_index("dom") % 2 == 0
    faces = jnp.concatenate(
        [jnp.where(even, upper_face, lower_face), jnp.where(even, lower_face, upper_face)]
    ).reshape(8, LANES)
    inside = [(i, i ^ 1) for i in range(n_dom)]
    across = [(i, i + 1) for i in range(1, n_dom - 1, 2)]
    across = across + [(j, i) for i, j in across]

    (info,) = call(
        functools.partial(info_kernel, n_dom=n_dom, cap=cap),
        [f32(n_dom, 4 * cap)],
        (owner, pair_master.reshape(1, -1), pair_normal),
    )
    info = lax.all_to_all(info, "dom", 0, 0, tiled=True)
    slave, slave_t, mortar_left, mortar_t, u, v, mass, mapped, neg_gap = call(
        functools.partial(prepare_kernel, n_dom=n_dom, cap=cap),
        [
            bf16(SLOTS, 12 * slaves),
            bf16(3 * slaves, 3 * SLOTS),
            bf16(3 * LANES, LANES),
            bf16(3 * LANES, LANES),
            field,
            field,
            field,
            f32(3 * masters, LANES),
            f32(SLOTS, LANES),
        ],
        (
            owner,
            pair_slave.reshape(1, -1),
            pair_normal,
            displacement,
            velocity,
            node_mass.reshape(1, -1),
            slave_nodes,
            master_nodes,
            slave_gap,
            mortar,
        ),
        us=3.0,
    )
    blocks = f32(n_dom, 2 * cap, LANES)
    slots = f32(SLOTS, LANES)
    out, m, owned = call(
        functools.partial(first_kernel, cap=cap), [blocks, slots, f32(SLOTS, 3 * masters)], (info, mapped, neg_gap)
    )
    for step in range(STEPS):
        recv = lax.all_to_all(out, "dom", 0, 0)
        (elastic,) = call(
            elastic_kernel,
            [field],
            (u, connectivity, modulus.reshape(1, -1), elem_stiffness),
            [pltpu.VMEM((24, connectivity.shape[1]), F32)],
            us=5.0,
        )
        if step == 0:
            master, master_t = call(turn_kernel, [bf16(SLOTS, 9 * masters), bf16(3 * masters, 3 * SLOTS)], (owned,))
        local, fa, fb = call(
            functools.partial(contact_kernel, cap=cap),
            [field, f32(3, 4, LANES), f32(3, 4, LANES)],
            (recv, neg_gap, slave_t, elastic, slave_nodes, faces),
            [pltpu.VMEM((3 * slaves, LANES), F32)],
            us=2.0,
        )
        ra = lax.ppermute(fa, "dom", inside)
        rb = lax.ppermute(fb, "dom", across)
        (negforce,) = call(
            functools.partial(master_kernel, cap=cap),
            [field],
            (recv, m, master_t, mortar_left, local, master_nodes),
            [pltpu.VMEM((3 * masters, LANES), F32)],
        )
        state = (negforce, ra, rb, faces, u, v, mass)
        if step < STEPS - 1:
            u, v, out, m, neg_gap = call(
                functools.partial(next_kernel, cap=cap),
                [field, field, blocks, slots, slots],
                (*state, slave_nodes, master_nodes, slave_gap, mortar_t, slave, master),
                us=2.0,
            )
        else:
            outs = [f32(*displacement.shape), f32(*velocity.shape)]
            u, v = call(last_kernel, outs, state)
    return (u, v)


def solution(mesh):
    return jax.shard_map(
        shards,
        mesh=mesh,
        in_specs=(
            P(None, ("groups", "dom")),
            P(None, ("groups", "dom")),
            P(("groups", "dom")),
            P(None, ("groups", "dom")),
            P(("groups", "dom")),
            P(),
            P(("groups", "dom"), None),
            P(("groups", "dom"), None),
            P(("groups", "dom"), None),
            P(("groups", "dom")),
            P(("groups", "dom"), None),
            P(("groups", "dom")),
            P(None, ("groups", "dom")),
            P(("groups", "dom")),
            P(("groups", "dom")),
            P(),
        ),
        out_specs=(P(None, ("groups", "dom")), P(None, ("groups", "dom"))),
        check_vma=False,
    )
```

```python
import functools

import jax
import jax.numpy as jnp
from jax import lax
from jax.experimental import pallas as pl
from jax.experimental.pallas import tpu as pltpu
from jax.sharding import PartitionSpec as P

LANES = 128
STEPS = 3
TIME_STEP = 0.1
SLOTS = 256
GROUP = 4

F32 = jnp.float32
BF16 = jnp.bfloat16
HIGH = lax.Precision.HIGHEST
NN = (((1,), (0,)), ((), ()))
NT = (((1,), (1,)), ((), ()))
TN = (((0,), (0,)), ((), ()))

MAIN = 16
ROWS = 56
FACTOR_ROWS = 112


def dot_exact(a, b, dims):
    return lax.dot_general(a, b, dims, precision=HIGH, preferred_element_type=F32)


def iota(shape, dim):
    return lax.broadcasted_iota(jnp.int32, shape, dim)


def field_row(c, h):
    return c * MAIN + h if h < MAIN else 3 * MAIN + c


def to_field(flat_ref, field_ref):
    field_ref[...] = jnp.zeros_like(field_ref)
    for c in range(3):
        for h in range(MAIN + 1):
            r = field_row(c, h)
            field_ref[r : r + 1, :] = flat_ref[c : c + 1, h * LANES : (h + 1) * LANES]


def from_field(field, flat_ref):
    for c in range(3):
        for h in range(MAIN + 1):
            r = field_row(c, h)
            flat_ref[c : c + 1, h * LANES : (h + 1) * LANES] = field[r : r + 1, :]


def gather8(field_ref, index):
    lane = index & (LANES - 1)
    row = index >> 7
    bits = [(row & (1 << q)) != 0 for q in range(4)]
    last = row >= MAIN
    found = []
    for c in range(3):
        values = []
        for h in range(MAIN + 1):
            r = field_row(c, h)
            table = jnp.broadcast_to(field_ref[r : r + 1, :], (8, LANES))
            values.append(jnp.take_along_axis(table, lane, axis=1, mode="promise_in_bounds"))
        tail = values.pop()
        for bit in bits:
            values = [jnp.where(bit, values[i + 1], values[i]) for i in range(0, len(values), 2)]
        found.append(jnp.where(last, tail, values[0]))
    return found


def value_factor(index, values):
    i16 = iota((MAIN, LANES), 0).astype(F32).astype(BF16)
    row = jnp.broadcast_to((index >> 7).astype(F32), (MAIN, LANES)).astype(BF16)
    zero = jnp.zeros((MAIN, LANES), BF16)
    here = i16 == row
    tail, out = zero, []
    for s in range(2):
        for c in range(3):
            high = values[c].astype(BF16).astype(F32)
            part = values[c] - high if s else high
            wide = jnp.broadcast_to(part, (MAIN, LANES)).astype(BF16)
            out.append(jnp.where(here, wide, zero))
            tail = jnp.where(i16 == jnp.full(i16.shape, c + 8 * s, BF16), wide, tail)
    out.append(jnp.where(row == jnp.full(row.shape, MAIN, BF16), tail, zero))
    return jnp.concatenate(out, axis=0)


def lane_factor(index):
    i128 = iota((LANES, LANES), 0).astype(F32).astype(BF16)
    lane = jnp.broadcast_to((index & (LANES - 1)).astype(F32), (LANES, LANES)).astype(BF16)
    return jnp.where(i128 == lane, jnp.ones((LANES, LANES), BF16), jnp.zeros((LANES, LANES), BF16))


def scatter(rows, total=None):
    for j in range(0, len(rows), GROUP):
        group = rows[j : j + GROUP]
        a = jnp.concatenate([value_factor(index, values) for index, values in group], axis=1)
        b = jnp.concatenate([lane_factor(index) for index, _ in group], axis=1)
        part = lax.dot_general(a, b, NT, preferred_element_type=F32)
        total = part if total is None else total + part
    return total


def factor_sum(total):
    m = 3 * MAIN
    return jnp.concatenate([total[:m] + total[m : 2 * m], total[2 * m : 2 * m + 8] + total[2 * m + 8 :]], axis=0)


def two_parts(x):
    high = x.astype(BF16)
    return high, (x - high.astype(F32)).astype(BF16)


def as_left(x, axis=1):
    high, low = two_parts(x)
    return jnp.concatenate([high, high, low], axis=axis)


def as_right(x, axis=0):
    high, low = two_parts(x)
    return jnp.concatenate([high, low, high], axis=axis)


def product(a, b):
    return lax.dot_general(a, b, NN, preferred_element_type=F32)


def take_slots(block_ref, first, cap):
    rows = slice(first, first + cap)
    if cap % 8 == 0:
        return block_ref[:, rows, :].reshape(-1, LANES)
    return jnp.concatenate([block_ref[o, rows, :] for o in range(block_ref.shape[0])], axis=0)


def put_slots(block_ref, first, cap, value):
    rows = slice(first, first + cap)
    if cap % 8 == 0:
        block_ref[:, rows, :] = value.reshape(-1, cap, LANES)
    else:
        for o in range(block_ref.shape[0]):
            block_ref[o, rows, :] = value[o * cap : (o + 1) * cap]


def send_slots(slots_ref, out_ref, first, sem):
    cap = slots_ref.shape[1]
    if cap % 8:
        put_slots(out_ref, first, cap, take_slots(slots_ref, 0, cap))
        return []
    copy = pltpu.make_async_copy(slots_ref, out_ref.at[:, pl.ds(first, cap), :], sem)
    copy.start()
    return [copy]


def ranks(owner, n_dom):
    n = owner.shape[1]
    at = (iota((n_dom, n), 0) == owner).astype(F32)
    before = (iota((n, n), 0) < iota((n, n), 1)).astype(F32)
    counts = lax.dot_general(at.astype(BF16), before.astype(BF16), NN, preferred_element_type=F32)
    return jnp.sum(at * counts, axis=0, keepdims=True), at


def info_kernel(owner_ref, master_ref, normal_ref, out_ref, *, n_dom, cap):
    rank, at = ranks(owner_ref[...], n_dom)
    q = iota((4 * cap, owner_ref.shape[1]), 0)
    which = lax.div(q, cap)
    value = jnp.broadcast_to(master_ref[...].astype(F32), q.shape)
    for c in range(3):
        value = jnp.where(which == c, jnp.broadcast_to(normal_ref[c : c + 1, :], q.shape), value)
    value = jnp.where(lax.rem(q, cap).astype(F32) == rank, value, 0.0)
    out_ref[...] = dot_exact(at, value, NT)


def gathered(field_ref, nodes_ref):
    blocks = [gather8(field_ref, nodes_ref[j : j + 8, :]) for j in range(0, nodes_ref.shape[0], 8)]
    return [jnp.concatenate([b[c] for b in blocks], axis=0) for c in range(3)]


def pair_values(u_ref, snodes_ref, mnodes_ref, gap_ref, mortar_t_ref):
    um = jnp.concatenate(gathered(u_ref, mnodes_ref), axis=0)
    us = jnp.concatenate([*gathered(u_ref, snodes_ref), gap_ref[...]], axis=0)
    return product(as_right(um, 1), mortar_t_ref[...]), as_right(us)


def prepare_kernel(
    owner_ref, pair_slave_ref, normal_ref, u_ref, v_ref, mass_ref, snodes_ref, mnodes_ref, gap_ref, mortar_ref,
    slave_ref, slave_t_ref, mortar_left_ref, mortar_t_ref, fu_ref, fv_ref, fm_ref, mapped_ref, neg_gap_ref, *, n_dom, cap,
):
    owner, patches = owner_ref[...], snodes_ref.shape[0]
    n = owner.shape[1]
    slot = owner.astype(F32) * cap + ranks(owner, n_dom)[0]
    place = (iota((SLOTS, n), 0).astype(F32) == slot).astype(F32)
    hit = iota((patches, n), 0) == pair_slave_ref[...]
    parts = [jnp.where(hit, jnp.broadcast_to(-normal_ref[c : c + 1, :], hit.shape), 0.0) for c in range(3)]
    slave_t_ref[...] = as_left(dot_exact(jnp.concatenate(parts, axis=0), place, NT))
    parts.append(jnp.where(hit, -1.0, 0.0))
    slave_ref[...] = as_left(dot_exact(place, jnp.concatenate(parts, axis=0), NT))
    mortar = mortar_ref[...]
    mortar_left_ref[...] = as_left(mortar, 0)
    mortar_t_ref[...] = as_left(mortar.T, 0)
    to_field(u_ref, fu_ref)
    to_field(v_ref, fv_ref)
    fm_ref[...] = jnp.ones_like(fm_ref)
    for c in range(3):
        for h in range(MAIN + 1):
            r = field_row(c, h)
            fm_ref[r : r + 1, :] = mass_ref[0:1, h * LANES : (h + 1) * LANES]
    mapped, parts = pair_values(fu_ref, snodes_ref, mnodes_ref, gap_ref, mortar_t_ref)
    mapped_ref[...] = mapped
    put_slots(neg_gap_ref, 0, cap, product(slave_ref[...], parts))


def first_kernel(info_ref, mapped_ref, neg_gap_ref, out_ref, m_ref, master_ref, sem_ref):
    n_dom, cap, _ = m_ref.shape
    masters = mapped_ref.shape[0] // 3
    copies = send_slots(neg_gap_ref, out_ref, cap, sem_ref.at[0])
    taken = jnp.concatenate([jnp.broadcast_to(info_ref[o : o + 1, :], (cap, 4 * cap)) for o in range(n_dom)], axis=0)
    mine = lax.rem(iota(taken.shape, 1), cap) == lax.rem(iota(taken.shape, 0), cap)
    f = lax.div(lax.rem(iota((8 * cap, 2 * LANES), 0), 4 * cap), cap)
    column = iota(f.shape, 1)
    spread = ((f == lax.div(column, masters)) & (column < LANES)) | ((f == 3) & (column >= LANES))
    both = product(jnp.concatenate(two_parts(jnp.where(mine, taken, 0.0)), axis=1), spread.astype(F32).astype(BF16))
    number = lax.rem(iota((SLOTS, LANES), 1), masters).astype(F32)
    owned = jnp.where(jnp.abs(both[:, LANES:] - number) < 0.5, both[:, :LANES], 0.0)[:, : 3 * masters]
    put_slots(m_ref, 0, cap, product(as_left(owned), as_right(mapped_ref[...])))
    copies += send_slots(m_ref, out_ref, 0, sem_ref.at[1])
    master_ref[...] = owned
    for copy in copies:
        copy.wait()


def turn_kernel(owned_ref, master_ref, master_t_ref):
    owned = owned_ref[...]
    master_ref[...] = as_left(owned)
    n = owned.shape[1]
    eye = (iota((n, n), 0) == iota((n, n), 1)).astype(F32)
    master_t_ref[...] = as_left(dot_exact(eye, owned, NT))


def elastic_kernel(u_ref, conn_ref, modulus_ref, stiff_ref, out_ref, ue_ref):
    tiles = conn_ref.shape[1] // LANES

    def gather_body(j, _):
        columns = pl.ds(pl.multiple_of(j * LANES, LANES), LANES)
        found = gather8(u_ref, conn_ref[:, columns])
        for c in range(3):
            ue_ref[c * 8 : (c + 1) * 8, columns] = found[c]
        return 0

    lax.fori_loop(0, tiles, gather_body, 0, unroll=4)
    ue_ref[...] = dot_exact(stiff_ref[...], ue_ref[...], NN) * modulus_ref[...]

    def body(j, total):
        columns = pl.ds(pl.multiple_of(j * LANES, LANES), LANES)
        rows = []
        for a in range(8):
            rows.append((conn_ref[a : a + 1, columns], [ue_ref[c * 8 + a : c * 8 + a + 1, columns] for c in range(3)]))
        return scatter(rows, total)

    total = lax.fori_loop(0, tiles, body, jnp.zeros((FACTOR_ROWS, LANES), F32), unroll=2)
    out_ref[...] = factor_sum(total)


def patch_rows(nodes_ref, values_ref):
    patches = nodes_ref.shape[0]
    return [
        (nodes_ref[r : r + 1, :], [values_ref[c * patches + r : c * patches + r + 1, :] for c in range(3)])
        for r in range(patches)
    ]


def face_rows(faces_ref, received_ref, first):
    return [(faces_ref[first + k : first + k + 1, :], [received_ref[c, k : k + 1, :] for c in range(3)]) for k in range(4)]


def contact_kernel(
    recv_ref, neg_gap_ref, slave_t_ref, elastic_ref, snodes_ref, faces_ref, local_ref, fa_ref, fb_ref, y_ref, *, cap
):
    press = jnp.maximum(take_slots(recv_ref, 0, cap) + take_slots(neg_gap_ref, 0, cap), 0.0)
    y_ref[...] = product(slave_t_ref[...], as_right(press))
    local_ref[...] = elastic_ref[...] + factor_sum(scatter(patch_rows(snodes_ref, y_ref)))
    found = gather8(local_ref, faces_ref[...])
    for c in range(3):
        fa_ref[c, :, :] = found[c][:4]
        fb_ref[c, :, :] = found[c][4:]


def master_kernel(recv_ref, m_ref, master_t_ref, mortar_ref, local_ref, mnodes_ref, faces_ref, ra_ref, out_ref, y_ref, *, cap):
    press = jnp.maximum(take_slots(m_ref, 0, cap) + take_slots(recv_ref, cap, cap), 0.0)
    summed = product(master_t_ref[...], as_right(press))
    y_ref[...] = product(as_right(summed, 1), mortar_ref[...])
    rows = patch_rows(mnodes_ref, y_ref) + face_rows(faces_ref, ra_ref, 0)
    out_ref[...] = local_ref[...] + factor_sum(scatter(rows))


def advance(negforce_ref, rb_ref, faces_ref, u_ref, v_ref, mass_ref):
    force = negforce_ref[...] + factor_sum(scatter(face_rows(faces_ref, rb_ref, 4)))
    v = v_ref[...] - TIME_STEP * force / mass_ref[...]
    return u_ref[...] + TIME_STEP * v, v


def next_kernel(
    negforce_ref, rb_ref, faces_ref, u_ref, v_ref, mass_ref, snodes_ref, mnodes_ref, gap_ref, mortar_t_ref, slave_ref,
    master_ref, nu_ref, nv_ref, out_ref, m_ref, neg_gap_ref, sem_ref,
):
    cap = m_ref.shape[1]
    u, v = advance(negforce_ref, rb_ref, faces_ref, u_ref, v_ref, mass_ref)
    nu_ref[...] = u
    nv_ref[...] = v
    mapped, parts = pair_values(nu_ref, snodes_ref, mnodes_ref, gap_ref, mortar_t_ref)
    put_slots(m_ref, 0, cap, product(master_ref[...], as_right(mapped)))
    copies = send_slots(m_ref, out_ref, 0, sem_ref.at[0])
    put_slots(neg_gap_ref, 0, cap, product(slave_ref[...], parts))
    copies += send_slots(neg_gap_ref, out_ref, cap, sem_ref.at[1])
    for copy in copies:
        copy.wait()


def last_kernel(negforce_ref, rb_ref, faces_ref, u_ref, v_ref, mass_ref, nu_ref, nv_ref):
    u, v = advance(negforce_ref, rb_ref, faces_ref, u_ref, v_ref, mass_ref)
    from_field(u, nu_ref)
    from_field(v, nv_ref)


def call(kernel, outs, args, scratch=(), us=1.0, far=()):
    vmem = pl.BlockSpec(memory_space=pltpu.VMEM)
    return pl.pallas_call(
        kernel,
        out_shape=outs,
        in_specs=[vmem] * len(args),
        out_specs=[pl.BlockSpec(memory_space=pl.ANY) if i in far else vmem for i in range(len(outs))],
        scratch_shapes=list(scratch),
        compiler_params=pltpu.CompilerParams(vmem_limit_bytes=40 << 20),
        cost_estimate=pl.CostEstimate(flops=int(us * 1e9), bytes_accessed=int(us * 3e6), transcendentals=0),
    )(*args)


def shards(
    displacement,
    velocity,
    node_mass,
    connectivity,
    modulus,
    elem_stiffness,
    slave_nodes,
    slave_gap,
    master_nodes,
    pair_slave,
    pair_owner,
    pair_master,
    pair_normal,
    lower_face,
    upper_face,
    mortar,
):
    n_dom = lax.axis_size("dom")
    cap = SLOTS // n_dom
    slaves, masters = slave_nodes.shape[0], master_nodes.shape[0]
    f32 = lambda *shape: jax.ShapeDtypeStruct(shape, F32)
    bf16 = lambda *shape: jax.ShapeDtypeStruct(shape, BF16)
    field = f32(ROWS, LANES)
    slots = f32(n_dom, cap, LANES)
    owner = pair_owner.reshape(1, -1)
    even = lax.axis_index("dom") % 2 == 0
    faces = jnp.concatenate(
        [jnp.where(even, upper_face, lower_face), jnp.where(even, lower_face, upper_face)]
    ).reshape(8, LANES)
    inside = [(i, i ^ 1) for i in range(n_dom)]
    across = [(i, i + 1) for i in range(1, n_dom - 1, 2)]
    across = across + [(j, i) for i, j in across]

    (info,) = call(
        functools.partial(info_kernel, n_dom=n_dom, cap=cap),
        [f32(n_dom, 4 * cap)],
        (owner, pair_master.reshape(1, -1), pair_normal),
    )
    info = lax.all_to_all(info, "dom", 0, 0, tiled=True)
    slave, slave_t, mortar_left, mortar_t, u, v, mass, mapped, neg_gap = call(
        functools.partial(prepare_kernel, n_dom=n_dom, cap=cap),
        [
            bf16(SLOTS, 12 * slaves),
            bf16(3 * slaves, 3 * SLOTS),
            bf16(3 * LANES, LANES),
            bf16(3 * LANES, LANES),
            field,
            field,
            field,
            f32(3 * masters, LANES),
            slots,
        ],
        (
            owner,
            pair_slave.reshape(1, -1),
            pair_normal,
            displacement,
            velocity,
            node_mass.reshape(1, -1),
            slave_nodes,
            master_nodes,
            slave_gap,
            mortar,
        ),
        us=3.0,
    )
    blocks = f32(n_dom, 2 * cap, LANES)
    sems = [pltpu.SemaphoreType.DMA((2,))]
    far = [] if cap % 8 else [0]
    out, m, owned = call(
        first_kernel, [blocks, slots, f32(SLOTS, 3 * masters)], (info, mapped, neg_gap), sems, far=far
    )
    far = [] if cap % 8 else [2]
    for step in range(STEPS):
        recv = lax.all_to_all(out, "dom", 0, 0)
        (elastic,) = call(
            elastic_kernel,
            [field],
            (u, connectivity, modulus.reshape(1, -1), elem_stiffness),
            [pltpu.VMEM((24, connectivity.shape[1]), F32)],
            us=5.0,
        )
        if step == 0:
            master, master_t = call(turn_kernel, [bf16(SLOTS, 9 * masters), bf16(3 * masters, 3 * SLOTS)], (owned,))
        local, fa, fb = call(
            functools.partial(contact_kernel, cap=cap),
            [field, f32(3, 4, LANES), f32(3, 4, LANES)],
            (recv, neg_gap, slave_t, elastic, slave_nodes, faces),
            [pltpu.VMEM((3 * slaves, LANES), F32)],
            us=2.0,
        )
        ra = lax.ppermute(fa, "dom", inside)
        rb = lax.ppermute(fb, "dom", across)
        (negforce,) = call(
            functools.partial(master_kernel, cap=cap),
            [field],
            (recv, m, master_t, mortar_left, local, master_nodes, faces, ra),
            [pltpu.VMEM((3 * masters, LANES), F32)],
        )
        state = (negforce, rb, faces, u, v, mass)
        if step < STEPS - 1:
            u, v, out, m, neg_gap = call(
                next_kernel,
                [field, field, blocks, slots, slots],
                (*state, slave_nodes, master_nodes, slave_gap, mortar_t, slave, master),
                sems,
                us=2.0,
                far=far,
            )
        else:
            outs = [f32(*displacement.shape), f32(*velocity.shape)]
            u, v = call(last_kernel, outs, state)
    return (u, v)


def solution(mesh):
    return jax.shard_map(
        shards,
        mesh=mesh,
        in_specs=(
            P(None, ("groups", "dom")),
            P(None, ("groups", "dom")),
            P(("groups", "dom")),
            P(None, ("groups", "dom")),
            P(("groups", "dom")),
            P(),
            P(("groups", "dom"), None),
            P(("groups", "dom"), None),
            P(("groups", "dom"), None),
            P(("groups", "dom")),
            P(("groups", "dom"), None),
            P(("groups", "dom")),
            P(None, ("groups", "dom")),
            P(("groups", "dom")),
            P(("groups", "dom")),
            P(),
        ),
        out_specs=(P(None, ("groups", "dom")), P(None, ("groups", "dom"))),
        check_vma=False,
    )
```

```python
import functools

import jax
import jax.numpy as jnp
from jax import lax
from jax.experimental import pallas as pl
from jax.experimental.pallas import tpu as pltpu
from jax.sharding import PartitionSpec as P

LANES = 128
STEPS = 3
TIME_STEP = 0.1
SLOTS = 256
GROUP = 4

F32 = jnp.float32
BF16 = jnp.bfloat16
HIGH = lax.Precision.HIGHEST
NN = (((1,), (0,)), ((), ()))
NT = (((1,), (1,)), ((), ()))
TN = (((0,), (0,)), ((), ()))

MAIN = 16
ROWS = 56
FACTOR_ROWS = 112


def dot_exact(a, b, dims):
    return lax.dot_general(a, b, dims, precision=HIGH, preferred_element_type=F32)


def iota(shape, dim):
    return lax.broadcasted_iota(jnp.int32, shape, dim)


def field_row(c, h):
    return c * MAIN + h if h < MAIN else 3 * MAIN + c


def to_field(flat_ref, field_ref):
    field_ref[...] = jnp.zeros_like(field_ref)
    for c in range(3):
        for h in range(MAIN + 1):
            r = field_row(c, h)
            field_ref[r : r + 1, :] = flat_ref[c : c + 1, h * LANES : (h + 1) * LANES]


def from_field(field, flat_ref):
    for c in range(3):
        for h in range(MAIN + 1):
            r = field_row(c, h)
            flat_ref[c : c + 1, h * LANES : (h + 1) * LANES] = field[r : r + 1, :]


def gather8(field_ref, index):
    lane = index & (LANES - 1)
    row = index >> 7
    bits = [(row & (1 << q)) != 0 for q in range(4)]
    last = row >= MAIN
    found = []
    for c in range(3):
        values = []
        for h in range(MAIN + 1):
            r = field_row(c, h)
            table = jnp.broadcast_to(field_ref[r : r + 1, :], (8, LANES))
            values.append(jnp.take_along_axis(table, lane, axis=1, mode="promise_in_bounds"))
        tail = values.pop()
        for bit in bits:
            values = [jnp.where(bit, values[i + 1], values[i]) for i in range(0, len(values), 2)]
        found.append(jnp.where(last, tail, values[0]))
    return found


def value_factor(index, values):
    i16 = iota((MAIN, LANES), 0).astype(F32).astype(BF16)
    row = jnp.broadcast_to((index >> 7).astype(F32), (MAIN, LANES)).astype(BF16)
    zero = jnp.zeros((MAIN, LANES), BF16)
    here = i16 == row
    tail, out = zero, []
    for s in range(2):
        for c in range(3):
            high = values[c].astype(BF16).astype(F32)
            part = values[c] - high if s else high
            wide = jnp.broadcast_to(part, (MAIN, LANES)).astype(BF16)
            out.append(jnp.where(here, wide, zero))
            tail = jnp.where(i16 == jnp.full(i16.shape, c + 8 * s, BF16), wide, tail)
    out.append(jnp.where(row == jnp.full(row.shape, MAIN, BF16), tail, zero))
    return jnp.concatenate(out, axis=0)


def lane_factor(index):
    i128 = iota((LANES, LANES), 0).astype(F32).astype(BF16)
    lane = jnp.broadcast_to((index & (LANES - 1)).astype(F32), (LANES, LANES)).astype(BF16)
    return jnp.where(i128 == lane, jnp.ones((LANES, LANES), BF16), jnp.zeros((LANES, LANES), BF16))


def scatter(rows, total=None):
    for j in range(0, len(rows), GROUP):
        group = rows[j : j + GROUP]
        a = jnp.concatenate([value_factor(index, values) for index, values in group], axis=1)
        b = jnp.concatenate([lane_factor(index) for index, _ in group], axis=1)
        part = lax.dot_general(a, b, NT, preferred_element_type=F32)
        total = part if total is None else total + part
    return total


def factor_sum(total):
    m = 3 * MAIN
    return jnp.concatenate([total[:m] + total[m : 2 * m], total[2 * m : 2 * m + 8] + total[2 * m + 8 :]], axis=0)


def two_parts(x):
    high = x.astype(BF16)
    return high, (x - high.astype(F32)).astype(BF16)


def as_left(x, axis=1):
    high, low = two_parts(x)
    return jnp.concatenate([high, high, low], axis=axis)


def as_right(x, axis=0):
    high, low = two_parts(x)
    return jnp.concatenate([high, low, high], axis=axis)


def product(a, b):
    return lax.dot_general(a, b, NN, preferred_element_type=F32)


def take_slots(block_ref, first, cap):
    rows = slice(first, first + cap)
    if cap % 8 == 0:
        return block_ref[:, rows, :].reshape(-1, LANES)
    return jnp.concatenate([block_ref[o, rows, :] for o in range(block_ref.shape[0])], axis=0)


def put_slots(block_ref, first, cap, value):
    rows = slice(first, first + cap)
    if cap % 8 == 0:
        block_ref[:, rows, :] = value.reshape(-1, cap, LANES)
    else:
        for o in range(block_ref.shape[0]):
            block_ref[o, rows, :] = value[o * cap : (o + 1) * cap]


def send_slots(slots_ref, out_ref, first, sem):
    cap = slots_ref.shape[1]
    if cap % 8:
        put_slots(out_ref, first, cap, take_slots(slots_ref, 0, cap))
        return []
    copy = pltpu.make_async_copy(slots_ref, out_ref.at[:, pl.ds(first, cap), :], sem)
    copy.start()
    return [copy]


def ranks(owner, n_dom):
    n = owner.shape[1]
    across = jnp.broadcast_to(owner.astype(F32), (n, n))
    same = (across.T == across) & (iota((n, n), 0) < iota((n, n), 1))
    return jnp.sum(same.astype(F32), axis=0, keepdims=True), (iota((n_dom, n), 0) == owner).astype(F32)


def info_kernel(owner_ref, master_ref, normal_ref, out_ref, *, n_dom, cap):
    rank, at = ranks(owner_ref[...], n_dom)
    q = iota((4 * cap, owner_ref.shape[1]), 0)
    which = lax.div(q, cap)
    value = jnp.broadcast_to(master_ref[...].astype(F32), q.shape)
    for c in range(3):
        value = jnp.where(which == c, jnp.broadcast_to(normal_ref[c : c + 1, :], q.shape), value)
    value = jnp.where(lax.rem(q, cap).astype(F32) == rank, value, 0.0)
    out_ref[...] = dot_exact(at, value, NT)


def gathered(field_ref, nodes_ref):
    blocks = [gather8(field_ref, nodes_ref[j : j + 8, :]) for j in range(0, nodes_ref.shape[0], 8)]
    return [jnp.concatenate([b[c] for b in blocks], axis=0) for c in range(3)]


def gathered_by_product(field, nodes_ref, out_ref):
    high, low = two_parts(field)
    m, patches = 3 * MAIN, nodes_ref.shape[0]
    tails = jnp.concatenate([high[m:].astype(F32), low[m:].astype(F32)], axis=0).astype(BF16)
    table = jnp.concatenate([high[:m], low[:m], tails], axis=0)
    for j in range(0, patches, GROUP):
        hot = jnp.concatenate([lane_factor(nodes_ref[j + k : j + k + 1, :]) for k in range(GROUP)], axis=1)
        found = lax.dot_general(table, hot, NN, preferred_element_type=F32)
        body, tail = found[:m] + found[m : 2 * m], found[2 * m : 2 * m + 8] + found[2 * m + 8 :]
        for k in range(GROUP):
            columns = slice(k * LANES, (k + 1) * LANES)
            upper = nodes_ref[j + k : j + k + 1, :] >> 7
            here = iota((MAIN, LANES), 0) == upper
            for c in range(3):
                picked = jnp.where(here, body[c * MAIN : (c + 1) * MAIN, columns], 0.0)
                row = jnp.sum(picked, axis=0, keepdims=True)
                out_ref[c * patches + j + k : c * patches + j + k + 1, :] = jnp.where(upper < MAIN, row, tail[c : c + 1, columns])


def pair_values(u_ref, snodes_ref, mnodes_ref, mortar_t_ref):
    um = jnp.concatenate(gathered(u_ref, mnodes_ref), axis=0)
    us = jnp.concatenate(gathered(u_ref, snodes_ref), axis=0)
    return product(as_right(um, 1), mortar_t_ref[...]), as_right(us)


def prepare_kernel(
    owner_ref, pair_slave_ref, normal_ref, u_ref, v_ref, mass_ref, snodes_ref, mnodes_ref, gap_ref, mortar_ref,
    slave_ref, slave_t_ref, mortar_left_ref, mortar_t_ref, fu_ref, fv_ref, fm_ref, mapped_ref, neg_gap_ref, start_ref, *, n_dom, cap,
):
    owner, patches = owner_ref[...], snodes_ref.shape[0]
    n = owner.shape[1]
    slot = owner.astype(F32) * cap + ranks(owner, n_dom)[0]
    place = (iota((SLOTS, n), 0).astype(F32) == slot).astype(F32)
    hit = iota((patches, n), 0) == pair_slave_ref[...]
    parts = [jnp.where(hit, jnp.broadcast_to(-normal_ref[c : c + 1, :], hit.shape), 0.0) for c in range(3)]
    slave_t_ref[...] = as_left(dot_exact(jnp.concatenate(parts, axis=0), place, NT))
    slave_ref[...] = as_left(dot_exact(place, jnp.concatenate(parts, axis=0), NT))
    start = dot_exact(dot_exact(place, jnp.where(hit, -1.0, 0.0), NT), gap_ref[...], NN)
    start_ref[...] = start
    mortar = mortar_ref[...]
    mortar_left_ref[...] = as_left(mortar, 0)
    mortar_t_ref[...] = as_left(mortar.T, 0)
    to_field(u_ref, fu_ref)
    to_field(v_ref, fv_ref)
    fm_ref[...] = jnp.ones_like(fm_ref)
    for c in range(3):
        for h in range(MAIN + 1):
            r = field_row(c, h)
            fm_ref[r : r + 1, :] = mass_ref[0:1, h * LANES : (h + 1) * LANES]
    mapped, parts = pair_values(fu_ref, snodes_ref, mnodes_ref, mortar_t_ref)
    mapped_ref[...] = mapped
    put_slots(neg_gap_ref, 0, cap, start + product(slave_ref[...], parts))


def first_kernel(info_ref, mapped_ref, neg_gap_ref, out_ref, m_ref, master_ref, sem_ref):
    n_dom, cap, _ = m_ref.shape
    masters = mapped_ref.shape[0] // 3
    copies = send_slots(neg_gap_ref, out_ref, cap, sem_ref.at[0])
    taken = jnp.concatenate([jnp.broadcast_to(info_ref[o : o + 1, :], (cap, 4 * cap)) for o in range(n_dom)], axis=0)
    mine = lax.rem(iota(taken.shape, 1), cap) == lax.rem(iota(taken.shape, 0), cap)
    f = lax.div(lax.rem(iota((8 * cap, 2 * LANES), 0), 4 * cap), cap)
    column = iota(f.shape, 1)
    spread = ((f == lax.div(column, masters)) & (column < LANES)) | ((f == 3) & (column >= LANES))
    both = product(jnp.concatenate(two_parts(jnp.where(mine, taken, 0.0)), axis=1), spread.astype(F32).astype(BF16))
    number = lax.rem(iota((SLOTS, LANES), 1), masters).astype(F32)
    owned = jnp.where(jnp.abs(both[:, LANES:] - number) < 0.5, both[:, :LANES], 0.0)[:, : 3 * masters]
    put_slots(m_ref, 0, cap, product(as_left(owned), as_right(mapped_ref[...])))
    copies += send_slots(m_ref, out_ref, 0, sem_ref.at[1])
    master_ref[...] = owned
    for copy in copies:
        copy.wait()


def turn_kernel(owned_ref, master_ref, master_t_ref):
    owned = owned_ref[...]
    master_ref[...] = as_left(owned)
    n = owned.shape[1]
    eye = (iota((n, n), 0) == iota((n, n), 1)).astype(F32)
    master_t_ref[...] = as_left(dot_exact(eye, owned, NT))


def elastic_kernel(u_ref, conn_ref, modulus_ref, stiff_ref, out_ref, ue_ref):
    tiles = conn_ref.shape[1] // LANES

    def gather_body(j, _):
        columns = pl.ds(pl.multiple_of(j * LANES, LANES), LANES)
        found = gather8(u_ref, conn_ref[:, columns])
        for c in range(3):
            ue_ref[c * 8 : (c + 1) * 8, columns] = found[c]
        return 0

    lax.fori_loop(0, tiles, gather_body, 0, unroll=4)
    ue_ref[...] = dot_exact(stiff_ref[...], ue_ref[...], NN) * modulus_ref[...]

    def body(j, total):
        columns = pl.ds(pl.multiple_of(j * LANES, LANES), LANES)
        rows = []
        for a in range(8):
            rows.append((conn_ref[a : a + 1, columns], [ue_ref[c * 8 + a : c * 8 + a + 1, columns] for c in range(3)]))
        return scatter(rows, total)

    total = lax.fori_loop(0, tiles, body, jnp.zeros((FACTOR_ROWS, LANES), F32), unroll=2)
    out_ref[...] = factor_sum(total)


def patch_rows(nodes_ref, values_ref):
    patches = nodes_ref.shape[0]
    return [
        (nodes_ref[r : r + 1, :], [values_ref[c * patches + r : c * patches + r + 1, :] for c in range(3)])
        for r in range(patches)
    ]


def face_rows(faces_ref, received_ref, first):
    return [(faces_ref[first + k : first + k + 1, :], [received_ref[c, k : k + 1, :] for c in range(3)]) for k in range(4)]


def contact_kernel(
    recv_ref, neg_gap_ref, slave_t_ref, elastic_ref, snodes_ref, faces_ref, local_ref, fa_ref, fb_ref, y_ref, *, cap
):
    press = jnp.maximum(take_slots(recv_ref, 0, cap) + take_slots(neg_gap_ref, 0, cap), 0.0)
    y_ref[...] = product(slave_t_ref[...], as_right(press))
    local_ref[...] = elastic_ref[...] + factor_sum(scatter(patch_rows(snodes_ref, y_ref)))
    found = gather8(local_ref, faces_ref[...])
    for c in range(3):
        fa_ref[c, :, :] = found[c][:4]
        fb_ref[c, :, :] = found[c][4:]


def master_kernel(recv_ref, m_ref, master_t_ref, mortar_ref, local_ref, mnodes_ref, faces_ref, ra_ref, out_ref, y_ref, *, cap):
    press = jnp.maximum(take_slots(m_ref, 0, cap) + take_slots(recv_ref, cap, cap), 0.0)
    summed = product(master_t_ref[...], as_right(press))
    y_ref[...] = product(as_right(summed, 1), mortar_ref[...])
    rows = patch_rows(mnodes_ref, y_ref) + face_rows(faces_ref, ra_ref, 0)
    out_ref[...] = local_ref[...] + factor_sum(scatter(rows))


def advance(negforce_ref, rb_ref, faces_ref, u_ref, v_ref, mass_ref):
    force = negforce_ref[...] + factor_sum(scatter(face_rows(faces_ref, rb_ref, 4)))
    v = v_ref[...] - TIME_STEP * force / mass_ref[...]
    return u_ref[...] + TIME_STEP * v, v


def next_kernel(
    negforce_ref, rb_ref, faces_ref, u_ref, v_ref, mass_ref, snodes_ref, mnodes_ref, start_ref, mortar_t_ref, slave_ref,
    master_ref, nu_ref, nv_ref, out_ref, m_ref, neg_gap_ref, sem_ref, um_ref,
):
    cap = m_ref.shape[1]
    u, v = advance(negforce_ref, rb_ref, faces_ref, u_ref, v_ref, mass_ref)
    nu_ref[...] = u
    nv_ref[...] = v
    gathered_by_product(u, mnodes_ref, um_ref)
    mapped = product(as_right(um_ref[...], 1), mortar_t_ref[...])
    parts = as_right(jnp.concatenate(gathered(nu_ref, snodes_ref), axis=0))
    put_slots(m_ref, 0, cap, product(master_ref[...], as_right(mapped)))
    copies = send_slots(m_ref, out_ref, 0, sem_ref.at[0])
    put_slots(neg_gap_ref, 0, cap, start_ref[...] + product(slave_ref[...], parts))
    copies += send_slots(neg_gap_ref, out_ref, cap, sem_ref.at[1])
    for copy in copies:
        copy.wait()


def last_kernel(negforce_ref, rb_ref, faces_ref, u_ref, v_ref, mass_ref, nu_ref, nv_ref):
    u, v = advance(negforce_ref, rb_ref, faces_ref, u_ref, v_ref, mass_ref)
    from_field(u, nu_ref)
    from_field(v, nv_ref)


def call(kernel, outs, args, scratch=(), us=1.0, far=()):
    vmem = pl.BlockSpec(memory_space=pltpu.VMEM)
    return pl.pallas_call(
        kernel,
        out_shape=outs,
        in_specs=[vmem] * len(args),
        out_specs=[pl.BlockSpec(memory_space=pl.ANY) if i in far else vmem for i in range(len(outs))],
        scratch_shapes=list(scratch),
        compiler_params=pltpu.CompilerParams(vmem_limit_bytes=40 << 20),
        cost_estimate=pl.CostEstimate(flops=int(us * 1e9), bytes_accessed=int(us * 3e6), transcendentals=0),
    )(*args)


def shards(
    displacement,
    velocity,
    node_mass,
    connectivity,
    modulus,
    elem_stiffness,
    slave_nodes,
    slave_gap,
    master_nodes,
    pair_slave,
    pair_owner,
    pair_master,
    pair_normal,
    lower_face,
    upper_face,
    mortar,
):
    n_dom = lax.axis_size("dom")
    cap = SLOTS // n_dom
    slaves, masters = slave_nodes.shape[0], master_nodes.shape[0]
    f32 = lambda *shape: jax.ShapeDtypeStruct(shape, F32)
    bf16 = lambda *shape: jax.ShapeDtypeStruct(shape, BF16)
    field = f32(ROWS, LANES)
    slots = f32(n_dom, cap, LANES)
    owner = pair_owner.reshape(1, -1)
    even = lax.axis_index("dom") % 2 == 0
    faces = jnp.concatenate(
        [jnp.where(even, upper_face, lower_face), jnp.where(even, lower_face, upper_face)]
    ).reshape(8, LANES)
    inside = [(i, i ^ 1) for i in range(n_dom)]
    across = [(i, i + 1) for i in range(1, n_dom - 1, 2)]
    across = across + [(j, i) for i, j in across]

    (info,) = call(
        functools.partial(info_kernel, n_dom=n_dom, cap=cap),
        [f32(n_dom, 4 * cap)],
        (owner, pair_master.reshape(1, -1), pair_normal),
    )
    info = lax.all_to_all(info, "dom", 0, 0, tiled=True)
    slave, slave_t, mortar_left, mortar_t, u, v, mass, mapped, neg_gap, start = call(
        functools.partial(prepare_kernel, n_dom=n_dom, cap=cap),
        [
            bf16(SLOTS, 9 * slaves),
            bf16(3 * slaves, 3 * SLOTS),
            bf16(3 * LANES, LANES),
            bf16(3 * LANES, LANES),
            field,
            field,
            field,
            f32(3 * masters, LANES),
            slots,
            f32(SLOTS, LANES),
        ],
        (
            owner,
            pair_slave.reshape(1, -1),
            pair_normal,
            displacement,
            velocity,
            node_mass.reshape(1, -1),
            slave_nodes,
            master_nodes,
            slave_gap,
            mortar,
        ),
        us=3.0,
    )
    blocks = f32(n_dom, 2 * cap, LANES)
    sems = [pltpu.SemaphoreType.DMA((2,))]
    far = [] if cap % 8 else [0]
    out, m, owned = call(
        first_kernel, [blocks, slots, f32(SLOTS, 3 * masters)], (info, mapped, neg_gap), sems, far=far
    )
    far = [] if cap % 8 else [2]
    for step in range(STEPS):
        recv = lax.all_to_all(out, "dom", 0, 0)
        (elastic,) = call(
            elastic_kernel,
            [field],
            (u, connectivity, modulus.reshape(1, -1), elem_stiffness),
            [pltpu.VMEM((24, connectivity.shape[1]), F32)],
            us=5.0,
        )
        if step == 0:
            master, master_t = call(turn_kernel, [bf16(SLOTS, 9 * masters), bf16(3 * masters, 3 * SLOTS)], (owned,))
        local, fa, fb = call(
            functools.partial(contact_kernel, cap=cap),
            [field, f32(3, 4, LANES), f32(3, 4, LANES)],
            (recv, neg_gap, slave_t, elastic, slave_nodes, faces),
            [pltpu.VMEM((3 * slaves, LANES), F32)],
            us=2.0,
        )
        ra = lax.ppermute(fa, "dom", inside)
        rb = lax.ppermute(fb, "dom", across)
        (negforce,) = call(
            functools.partial(master_kernel, cap=cap),
            [field],
            (recv, m, master_t, mortar_left, local, master_nodes, faces, ra),
            [pltpu.VMEM((3 * masters, LANES), F32)],
        )
        state = (negforce, rb, faces, u, v, mass)
        if step < STEPS - 1:
            u, v, out, m, neg_gap = call(
                next_kernel,
                [field, field, blocks, slots, slots],
                (*state, slave_nodes, master_nodes, start, mortar_t, slave, master),
                [*sems, pltpu.VMEM((3 * masters, LANES), F32)],
                us=2.0,
                far=far,
            )
        else:
            outs = [f32(*displacement.shape), f32(*velocity.shape)]
            u, v = call(last_kernel, outs, state)
    return (u, v)


def solution(mesh):
    return jax.shard_map(
        shards,
        mesh=mesh,
        in_specs=(
            P(None, ("groups", "dom")),
            P(None, ("groups", "dom")),
            P(("groups", "dom")),
            P(None, ("groups", "dom")),
            P(("groups", "dom")),
            P(),
            P(("groups", "dom"), None),
            P(("groups", "dom"), None),
            P(("groups", "dom"), None),
            P(("groups", "dom")),
            P(("groups", "dom"), None),
            P(("groups", "dom")),
            P(None, ("groups", "dom")),
            P(("groups", "dom")),
            P(("groups", "dom")),
            P(),
        ),
        out_specs=(P(None, ("groups", "dom")), P(None, ("groups", "dom"))),
        check_vma=False,
    )
```

```python
import functools

import jax
import jax.numpy as jnp
from jax import lax
from jax.experimental import pallas as pl
from jax.experimental.pallas import tpu as pltpu
from jax.sharding import PartitionSpec as P

LANES = 128
STEPS = 3
TIME_STEP = 0.1
SLOTS = 256
GROUP = 4
WIDE = 8

F32 = jnp.float32
BF16 = jnp.bfloat16
HIGH = lax.Precision.HIGHEST
NN = (((1,), (0,)), ((), ()))
NT = (((1,), (1,)), ((), ()))
TN = (((0,), (0,)), ((), ()))

MAIN = 16
ROWS = 56
FACTOR_ROWS = 112


def dot_exact(a, b, dims):
    return lax.dot_general(a, b, dims, precision=HIGH, preferred_element_type=F32)


def iota(shape, dim):
    return lax.broadcasted_iota(jnp.int32, shape, dim)


def field_row(c, h):
    return c * MAIN + h if h < MAIN else 3 * MAIN + c


def to_field(flat_ref, field_ref):
    field_ref[...] = jnp.zeros_like(field_ref)
    for c in range(3):
        for h in range(MAIN + 1):
            r = field_row(c, h)
            field_ref[r : r + 1, :] = flat_ref[c : c + 1, h * LANES : (h + 1) * LANES]


def from_field(field, flat_ref):
    for c in range(3):
        for h in range(MAIN + 1):
            r = field_row(c, h)
            flat_ref[c : c + 1, h * LANES : (h + 1) * LANES] = field[r : r + 1, :]


def gather8(field_ref, index):
    lane = index & (LANES - 1)
    row = index >> 7
    bits = [(row & (1 << q)) != 0 for q in range(4)]
    last = row >= MAIN
    found = []
    for c in range(3):
        values = []
        for h in range(MAIN + 1):
            r = field_row(c, h)
            table = jnp.broadcast_to(field_ref[r : r + 1, :], (8, LANES))
            values.append(jnp.take_along_axis(table, lane, axis=1, mode="promise_in_bounds"))
        tail = values.pop()
        for bit in bits:
            values = [jnp.where(bit, values[i + 1], values[i]) for i in range(0, len(values), 2)]
        found.append(jnp.where(last, tail, values[0]))
    return found


def value_factor(index, values):
    i16 = iota((MAIN, LANES), 0).astype(F32).astype(BF16)
    row = jnp.broadcast_to((index >> 7).astype(F32), (MAIN, LANES)).astype(BF16)
    zero = jnp.zeros((MAIN, LANES), BF16)
    here = i16 == row
    tail, out = zero, []
    for s in range(2):
        for c in range(3):
            high = values[c].astype(BF16).astype(F32)
            part = values[c] - high if s else high
            wide = jnp.broadcast_to(part, (MAIN, LANES)).astype(BF16)
            out.append(jnp.where(here, wide, zero))
            tail = jnp.where(i16 == jnp.full(i16.shape, c + 8 * s, BF16), wide, tail)
    out.append(jnp.where(row == jnp.full(row.shape, MAIN, BF16), tail, zero))
    return jnp.concatenate(out, axis=0)


def lane_factor(index):
    i128 = iota((LANES, LANES), 0).astype(F32).astype(BF16)
    lane = jnp.broadcast_to((index & (LANES - 1)).astype(F32), (LANES, LANES)).astype(BF16)
    return jnp.where(i128 == lane, jnp.ones((LANES, LANES), BF16), jnp.zeros((LANES, LANES), BF16))


def scatter(rows, total=None):
    for j in range(0, len(rows), GROUP):
        group = rows[j : j + GROUP]
        a = jnp.concatenate([value_factor(index, values) for index, values in group], axis=1)
        b = jnp.concatenate([lane_factor(index) for index, _ in group], axis=1)
        part = lax.dot_general(a, b, NT, preferred_element_type=F32)
        total = part if total is None else total + part
    return total


def factor_sum(total):
    m = 3 * MAIN
    return jnp.concatenate([total[:m] + total[m : 2 * m], total[2 * m : 2 * m + 8] + total[2 * m + 8 :]], axis=0)


def two_parts(x):
    high = x.astype(BF16)
    return high, (x - high.astype(F32)).astype(BF16)


def as_left(x, axis=1):
    high, low = two_parts(x)
    return jnp.concatenate([high, high, low], axis=axis)


def as_right(x, axis=0):
    high, low = two_parts(x)
    return jnp.concatenate([high, low, high], axis=axis)


def product(a, b):
    return lax.dot_general(a, b, NN, preferred_element_type=F32)


def take_slots(block_ref, first, cap):
    rows = slice(first, first + cap)
    if cap % 8 == 0:
        return block_ref[:, rows, :].reshape(-1, LANES)
    return jnp.concatenate([block_ref[o, rows, :] for o in range(block_ref.shape[0])], axis=0)


def put_slots(block_ref, first, cap, value):
    rows = slice(first, first + cap)
    if cap % 8 == 0:
        block_ref[:, rows, :] = value.reshape(-1, cap, LANES)
    else:
        for o in range(block_ref.shape[0]):
            block_ref[o, rows, :] = value[o * cap : (o + 1) * cap]


def send_slots(slots_ref, out_ref, first, sem):
    cap = slots_ref.shape[1]
    if cap % 8:
        put_slots(out_ref, first, cap, take_slots(slots_ref, 0, cap))
        return []
    copy = pltpu.make_async_copy(slots_ref, out_ref.at[:, pl.ds(first, cap), :], sem)
    copy.start()
    return [copy]


def ranks(owner, n_dom):
    n = owner.shape[1]
    across = jnp.broadcast_to(owner.astype(F32), (n, n))
    same = (across.T == across) & (iota((n, n), 0) < iota((n, n), 1))
    return jnp.sum(same.astype(F32), axis=0, keepdims=True), (iota((n_dom, n), 0) == owner).astype(F32)


def info_kernel(owner_ref, master_ref, normal_ref, out_ref, *, n_dom, cap):
    rank, at = ranks(owner_ref[...], n_dom)
    q = iota((4 * cap, owner_ref.shape[1]), 0)
    which = lax.div(q, cap)
    value = jnp.broadcast_to(master_ref[...].astype(F32), q.shape)
    for c in range(3):
        value = jnp.where(which == c, jnp.broadcast_to(normal_ref[c : c + 1, :], q.shape), value)
    value = jnp.where(lax.rem(q, cap).astype(F32) == rank, value, 0.0)
    out_ref[...] = dot_exact(at, value, NT)


def gathered(field_ref, nodes_ref):
    blocks = [gather8(field_ref, nodes_ref[j : j + 8, :]) for j in range(0, nodes_ref.shape[0], 8)]
    return [jnp.concatenate([b[c] for b in blocks], axis=0) for c in range(3)]


def gathered_by_product(field, nodes_ref, out_ref):
    high, low = two_parts(field)
    m, patches = 3 * MAIN, nodes_ref.shape[0]
    tails = jnp.concatenate([high[m:].astype(F32), low[m:].astype(F32)], axis=0).astype(BF16)
    table = jnp.concatenate([high[:m], low[:m], tails], axis=0)
    for j in range(0, patches, WIDE):
        hot = jnp.concatenate([lane_factor(nodes_ref[j + k : j + k + 1, :]) for k in range(WIDE)], axis=1)
        found = lax.dot_general(table, hot, NN, preferred_element_type=F32)
        body, tail = found[:m] + found[m : 2 * m], found[2 * m : 2 * m + 8] + found[2 * m + 8 :]
        for k in range(WIDE):
            columns = slice(k * LANES, (k + 1) * LANES)
            upper = nodes_ref[j + k : j + k + 1, :] >> 7
            here = iota((MAIN, LANES), 0) == upper
            for c in range(3):
                picked = jnp.where(here, body[c * MAIN : (c + 1) * MAIN, columns], 0.0)
                row = jnp.sum(picked, axis=0, keepdims=True)
                out_ref[c * patches + j + k : c * patches + j + k + 1, :] = jnp.where(upper < MAIN, row, tail[c : c + 1, columns])


def pair_values(u_ref, snodes_ref, mnodes_ref, mortar_t_ref):
    um = jnp.concatenate(gathered(u_ref, mnodes_ref), axis=0)
    us = jnp.concatenate(gathered(u_ref, snodes_ref), axis=0)
    return product(as_right(um, 1), mortar_t_ref[...]), as_right(us)


def prepare_kernel(
    owner_ref, pair_slave_ref, normal_ref, u_ref, v_ref, mass_ref, snodes_ref, mnodes_ref, gap_ref, mortar_ref,
    slave_ref, slave_t_ref, mortar_left_ref, mortar_t_ref, fu_ref, fv_ref, fm_ref, mapped_ref, neg_gap_ref, start_ref, *, n_dom, cap,
):
    owner, patches = owner_ref[...], snodes_ref.shape[0]
    n = owner.shape[1]
    slot = owner.astype(F32) * cap + ranks(owner, n_dom)[0]
    place = (iota((SLOTS, n), 0).astype(F32) == slot).astype(F32)
    hit = iota((patches, n), 0) == pair_slave_ref[...]
    parts = [jnp.where(hit, jnp.broadcast_to(-normal_ref[c : c + 1, :], hit.shape), 0.0) for c in range(3)]
    slave_t_ref[...] = as_left(dot_exact(jnp.concatenate(parts, axis=0), place, NT))
    slave_ref[...] = as_left(dot_exact(place, jnp.concatenate(parts, axis=0), NT))
    start = dot_exact(dot_exact(place, jnp.where(hit, -1.0, 0.0), NT), gap_ref[...], NN)
    start_ref[...] = start
    mortar = mortar_ref[...]
    mortar_left_ref[...] = as_left(mortar, 0)
    mortar_t_ref[...] = as_left(mortar.T, 0)
    to_field(u_ref, fu_ref)
    to_field(v_ref, fv_ref)
    fm_ref[...] = jnp.ones_like(fm_ref)
    for c in range(3):
        for h in range(MAIN + 1):
            r = field_row(c, h)
            fm_ref[r : r + 1, :] = TIME_STEP / mass_ref[0:1, h * LANES : (h + 1) * LANES]
    mapped, parts = pair_values(fu_ref, snodes_ref, mnodes_ref, mortar_t_ref)
    mapped_ref[...] = mapped
    put_slots(neg_gap_ref, 0, cap, start + product(slave_ref[...], parts))


def first_kernel(info_ref, mapped_ref, neg_gap_ref, out_ref, m_ref, master_ref, sem_ref):
    n_dom, cap, _ = m_ref.shape
    masters = mapped_ref.shape[0] // 3
    copies = send_slots(neg_gap_ref, out_ref, cap, sem_ref.at[0])
    taken = jnp.concatenate([jnp.broadcast_to(info_ref[o : o + 1, :], (cap, 4 * cap)) for o in range(n_dom)], axis=0)
    mine = lax.rem(iota(taken.shape, 1), cap) == lax.rem(iota(taken.shape, 0), cap)
    f = lax.div(lax.rem(iota((8 * cap, 2 * LANES), 0), 4 * cap), cap)
    column = iota(f.shape, 1)
    spread = ((f == lax.div(column, masters)) & (column < LANES)) | ((f == 3) & (column >= LANES))
    both = product(jnp.concatenate(two_parts(jnp.where(mine, taken, 0.0)), axis=1), spread.astype(F32).astype(BF16))
    number = lax.rem(iota((SLOTS, LANES), 1), masters).astype(F32)
    owned = jnp.where(jnp.abs(both[:, LANES:] - number) < 0.5, both[:, :LANES], 0.0)[:, : 3 * masters]
    put_slots(m_ref, 0, cap, product(as_left(owned), as_right(mapped_ref[...])))
    copies += send_slots(m_ref, out_ref, 0, sem_ref.at[1])
    master_ref[...] = owned
    for copy in copies:
        copy.wait()


def turn_kernel(owned_ref, master_ref, master_t_ref):
    owned = owned_ref[...]
    master_ref[...] = as_left(owned)
    n = owned.shape[1]
    eye = (iota((n, n), 0) == iota((n, n), 1)).astype(F32)
    master_t_ref[...] = as_left(dot_exact(eye, owned, NT))


def elastic_kernel(u_ref, conn_ref, modulus_ref, stiff_ref, out_ref, ue_ref):
    tiles = conn_ref.shape[1] // LANES

    def gather_body(j, _):
        columns = pl.ds(pl.multiple_of(j * LANES, LANES), LANES)
        found = gather8(u_ref, conn_ref[:, columns])
        for c in range(3):
            ue_ref[c * 8 : (c + 1) * 8, columns] = found[c]
        return 0

    lax.fori_loop(0, tiles, gather_body, 0, unroll=4)
    ue_ref[...] = dot_exact(stiff_ref[...], ue_ref[...], NN) * modulus_ref[...]

    def body(j, total):
        columns = pl.ds(pl.multiple_of(j * LANES, LANES), LANES)
        rows = []
        for a in range(8):
            rows.append((conn_ref[a : a + 1, columns], [ue_ref[c * 8 + a : c * 8 + a + 1, columns] for c in range(3)]))
        return scatter(rows, total)

    total = lax.fori_loop(0, tiles, body, jnp.zeros((FACTOR_ROWS, LANES), F32), unroll=2)
    out_ref[...] = factor_sum(total)


def patch_rows(nodes_ref, values_ref):
    patches = nodes_ref.shape[0]
    return [
        (nodes_ref[r : r + 1, :], [values_ref[c * patches + r : c * patches + r + 1, :] for c in range(3)])
        for r in range(patches)
    ]


def face_rows(faces_ref, received_ref, first):
    return [(faces_ref[first + k : first + k + 1, :], [received_ref[c, k : k + 1, :] for c in range(3)]) for k in range(4)]


def contact_kernel(
    recv_ref, neg_gap_ref, slave_t_ref, elastic_ref, snodes_ref, faces_ref, local_ref, fa_ref, fb_ref, y_ref, *, cap
):
    press = jnp.maximum(take_slots(recv_ref, 0, cap) + take_slots(neg_gap_ref, 0, cap), 0.0)
    y_ref[...] = product(slave_t_ref[...], as_right(press))
    local_ref[...] = elastic_ref[...] + factor_sum(scatter(patch_rows(snodes_ref, y_ref)))
    found = gather8(local_ref, faces_ref[...])
    for c in range(3):
        fa_ref[c, :, :] = found[c][:4]
        fb_ref[c, :, :] = found[c][4:]


def master_kernel(recv_ref, m_ref, master_t_ref, mortar_ref, local_ref, mnodes_ref, faces_ref, ra_ref, out_ref, y_ref, *, cap):
    press = jnp.maximum(take_slots(m_ref, 0, cap) + take_slots(recv_ref, cap, cap), 0.0)
    summed = product(master_t_ref[...], as_right(press))
    y_ref[...] = product(as_right(summed, 1), mortar_ref[...])
    rows = patch_rows(mnodes_ref, y_ref) + face_rows(faces_ref, ra_ref, 0)
    out_ref[...] = local_ref[...] + factor_sum(scatter(rows))


def advance(negforce_ref, rb_ref, faces_ref, u_ref, v_ref, rate_ref):
    force = negforce_ref[...] + factor_sum(scatter(face_rows(faces_ref, rb_ref, 4)))
    v = v_ref[...] - force * rate_ref[...]
    return u_ref[...] + TIME_STEP * v, v


def next_kernel(
    negforce_ref, rb_ref, faces_ref, u_ref, v_ref, mass_ref, snodes_ref, mnodes_ref, start_ref, mortar_t_ref, slave_ref,
    master_ref, nu_ref, nv_ref, out_ref, m_ref, neg_gap_ref, sem_ref, um_ref,
):
    cap = m_ref.shape[1]
    u, v = advance(negforce_ref, rb_ref, faces_ref, u_ref, v_ref, mass_ref)
    nu_ref[...] = u
    nv_ref[...] = v
    gathered_by_product(u, mnodes_ref, um_ref)
    mapped = product(as_right(um_ref[...], 1), mortar_t_ref[...])
    parts = as_right(jnp.concatenate(gathered(nu_ref, snodes_ref), axis=0))
    put_slots(m_ref, 0, cap, product(master_ref[...], as_right(mapped)))
    copies = send_slots(m_ref, out_ref, 0, sem_ref.at[0])
    put_slots(neg_gap_ref, 0, cap, start_ref[...] + product(slave_ref[...], parts))
    copies += send_slots(neg_gap_ref, out_ref, cap, sem_ref.at[1])
    for copy in copies:
        copy.wait()


def last_kernel(negforce_ref, rb_ref, faces_ref, u_ref, v_ref, mass_ref, nu_ref, nv_ref):
    u, v = advance(negforce_ref, rb_ref, faces_ref, u_ref, v_ref, mass_ref)
    from_field(u, nu_ref)
    from_field(v, nv_ref)


def call(kernel, outs, args, scratch=(), us=1.0, far=()):
    vmem = pl.BlockSpec(memory_space=pltpu.VMEM)
    return pl.pallas_call(
        kernel,
        out_shape=outs,
        in_specs=[vmem] * len(args),
        out_specs=[pl.BlockSpec(memory_space=pl.ANY) if i in far else vmem for i in range(len(outs))],
        scratch_shapes=list(scratch),
        compiler_params=pltpu.CompilerParams(vmem_limit_bytes=40 << 20),
        cost_estimate=pl.CostEstimate(flops=int(us * 1e9), bytes_accessed=int(us * 3e6), transcendentals=0),
    )(*args)


def shards(
    displacement,
    velocity,
    node_mass,
    connectivity,
    modulus,
    elem_stiffness,
    slave_nodes,
    slave_gap,
    master_nodes,
    pair_slave,
    pair_owner,
    pair_master,
    pair_normal,
    lower_face,
    upper_face,
    mortar,
):
    n_dom = lax.axis_size("dom")
    cap = SLOTS // n_dom
    slaves, masters = slave_nodes.shape[0], master_nodes.shape[0]
    f32 = lambda *shape: jax.ShapeDtypeStruct(shape, F32)
    bf16 = lambda *shape: jax.ShapeDtypeStruct(shape, BF16)
    field = f32(ROWS, LANES)
    slots = f32(n_dom, cap, LANES)
    owner = pair_owner.reshape(1, -1)
    even = lax.axis_index("dom") % 2 == 0
    faces = jnp.concatenate(
        [jnp.where(even, upper_face, lower_face), jnp.where(even, lower_face, upper_face)]
    ).reshape(8, LANES)
    inside = [(i, i ^ 1) for i in range(n_dom)]
    across = [(i, i + 1) for i in range(1, n_dom - 1, 2)]
    across = across + [(j, i) for i, j in across]

    (info,) = call(
        functools.partial(info_kernel, n_dom=n_dom, cap=cap),
        [f32(n_dom, 4 * cap)],
        (owner, pair_master.reshape(1, -1), pair_normal),
    )
    info = lax.all_to_all(info, "dom", 0, 0, tiled=True)
    slave, slave_t, mortar_left, mortar_t, u, v, mass, mapped, neg_gap, start = call(
        functools.partial(prepare_kernel, n_dom=n_dom, cap=cap),
        [
            bf16(SLOTS, 9 * slaves),
            bf16(3 * slaves, 3 * SLOTS),
            bf16(3 * LANES, LANES),
            bf16(3 * LANES, LANES),
            field,
            field,
            field,
            f32(3 * masters, LANES),
            slots,
            f32(SLOTS, LANES),
        ],
        (
            owner,
            pair_slave.reshape(1, -1),
            pair_normal,
            displacement,
            velocity,
            node_mass.reshape(1, -1),
            slave_nodes,
            master_nodes,
            slave_gap,
            mortar,
        ),
        us=3.0,
    )
    blocks = f32(n_dom, 2 * cap, LANES)
    sems = [pltpu.SemaphoreType.DMA((2,))]
    far = [] if cap % 8 else [0]
    out, m, owned = call(
        first_kernel, [blocks, slots, f32(SLOTS, 3 * masters)], (info, mapped, neg_gap), sems, far=far
    )
    far = [] if cap % 8 else [2]
    for step in range(STEPS):
        recv = lax.all_to_all(out, "dom", 0, 0)
        (elastic,) = call(
            elastic_kernel,
            [field],
            (u, connectivity, modulus.reshape(1, -1), elem_stiffness),
            [pltpu.VMEM((24, connectivity.shape[1]), F32)],
            us=5.0,
        )
        if step == 0:
            master, master_t = call(turn_kernel, [bf16(SLOTS, 9 * masters), bf16(3 * masters, 3 * SLOTS)], (owned,))
        local, fa, fb = call(
            functools.partial(contact_kernel, cap=cap),
            [field, f32(3, 4, LANES), f32(3, 4, LANES)],
            (recv, neg_gap, slave_t, elastic, slave_nodes, faces),
            [pltpu.VMEM((3 * slaves, LANES), F32)],
            us=2.0,
        )
        ra = lax.ppermute(fa, "dom", inside)
        rb = lax.ppermute(fb, "dom", across)
        (negforce,) = call(
            functools.partial(master_kernel, cap=cap),
            [field],
            (recv, m, master_t, mortar_left, local, master_nodes, faces, ra),
            [pltpu.VMEM((3 * masters, LANES), F32)],
        )
        state = (negforce, rb, faces, u, v, mass)
        if step < STEPS - 1:
            u, v, out, m, neg_gap = call(
                next_kernel,
                [field, field, blocks, slots, slots],
                (*state, slave_nodes, master_nodes, start, mortar_t, slave, master),
                [*sems, pltpu.VMEM((3 * masters, LANES), F32)],
                us=2.0,
                far=far,
            )
        else:
            outs = [f32(*displacement.shape), f32(*velocity.shape)]
            u, v = call(last_kernel, outs, state)
    return (u, v)


def solution(mesh):
    return jax.shard_map(
        shards,
        mesh=mesh,
        in_specs=(
            P(None, ("groups", "dom")),
            P(None, ("groups", "dom")),
            P(("groups", "dom")),
            P(None, ("groups", "dom")),
            P(("groups", "dom")),
            P(),
            P(("groups", "dom"), None),
            P(("groups", "dom"), None),
            P(("groups", "dom"), None),
            P(("groups", "dom")),
            P(("groups", "dom"), None),
            P(("groups", "dom")),
            P(None, ("groups", "dom")),
            P(("groups", "dom")),
            P(("groups", "dom")),
            P(),
        ),
        out_specs=(P(None, ("groups", "dom")), P(None, ("groups", "dom"))),
        check_vma=False,
    )
```
